256 devices in a mesh: fin: 16 (over y, z_lo), fout: 16 (over x, z_hi, core).
Axes of the slice: x: 4, y: 4, z: 8 (z_hi: 2, z_lo: 4; z = z_hi * 4 + z_lo), core: 2. Of those that a mesh axis runs over, the one named last changes fastest.
Arguments:
- tokens: bfloat16 [256, 6144], P(None, 'fin'), may hold values from -60 to 60
- norm_gain: float32 [6144], P('fin'), may hold values from 0.1 to 1.9
- attend_weight: bfloat16 [3, 6144, 6144], P(None, 'fin', 'fout'), may hold values from -0.078125 to 0.078125
- up_weight: bfloat16 [6144, 24576], P('fin', 'fout'), may hold values from -0.078125 to 0.078125
- out_weight: bfloat16 [6144, 6144], P('fout', 'fin'), may hold values from -0.078125 to 0.078125
- down_weight: bfloat16 [24576, 6144], P('fout', 'fin'), may hold values from -0.0390625 to 0.0390625
- upstream: bfloat16 [256, 6144], P(None, 'fin'), may hold values from -6 to 6
Outputs:
- layer_out: bfloat16 [256, 6144], P(None, 'fin')
- tokens_grad: bfloat16 [256, 6144], P(None, 'fin')
- gain_grad: float32 [6144], P('fin')
- attend_grad: bfloat16 [3, 6144, 6144], P(None, 'fin', 'fout')
- up_grad: bfloat16 [6144, 24576], P('fin', 'fout')
- out_grad: bfloat16 [6144, 6144], P('fout', 'fin')
- down_grad: bfloat16 [24576, 6144], P('fout', 'fin')
The draws below stay inside these ranges and needn't reach their ends.
All inputs are finite; a program needn't handle non-finite values.
Results may differ from the reference program's by a relative error of at most 0.024.
Values may be sent and summed in bfloat16 or wider, within the bound.
A program may use at most 64 MiB of HBM per device.

```python
import math
import jax
import jax.numpy as jnp
from jax import lax

D = 6144
FF = 24576
HEADS = 48
HEAD_DIM = 128
SEQ = 256
IMG = 1
TOKENS = 256


def draw_tokens(key, part):
    key = jax.random.fold_in(key, 17)
    base_key, column_key, row_key = jax.random.split(key, 3)
    position = jnp.arange(D, dtype=jnp.float32) / D
    columns = 0.15 * jnp.exp(position * math.log(3.0) + jax.random.uniform(column_key, (D,), jnp.float32, 0.0, math.log(10.0)))
    row_scales = jnp.exp(jax.random.uniform(row_key, (TOKENS, 1), jnp.float32, math.log(0.3), math.log(3.0)))
    values_base = jax.random.truncated_normal(base_key, -4.0, 4.0, (TOKENS, D), jnp.float32)
    return (values_base * row_scales * columns[None, :]).astype(jnp.bfloat16)


def with_spikes(drawn, stream_key, source, target, parts, factor):
    def block_of(axis_at):
        return (jnp.arange(drawn.shape[axis_at]) // (drawn.shape[axis_at] // parts)).reshape((-1,) + (1,) * (drawn.ndim - 1 - axis_at))

    near = jax.random.permutation(stream_key, parts)[block_of(target)]
    far = (block_of(target) + parts // 2) % parts
    return jnp.where((block_of(source) == near) | (block_of(source) == far), factor * drawn, drawn)


def block_levels(key, extent, shards, least, top_value):
    level, own = 1.0, jax.random.fold_in(key, 6)
    for dim, shards_of in shards:
        steps = jnp.exp(jax.random.uniform(jax.random.fold_in(own, dim), (shards_of,), jnp.float32, least / len(shards), top_value / len(shards)))
        level = level * jnp.repeat(steps, extent[dim] // shards_of).reshape([-1 if axis == dim else 1 for axis in range(len(extent))])
    return level


def gaussian(key, shape, spread, most, cuts=(), held_as=jnp.bfloat16):
    level = block_levels(key, shape, cuts, -0.22, 0.18) if cuts else 1.0
    values = jax.random.normal(key, shape, jnp.float32) * spread * level
    return jnp.minimum(jnp.maximum(values, -most), most).astype(held_as)


def heavy_noise(rng, shape, scale, most, cuts, heavy, held_as=jnp.bfloat16):
    result = scale * jax.random.normal(rng, shape, jnp.float32)
    if cuts:
        result = result * block_levels(rng, shape, cuts, -0.22, 0.18)
    return jnp.clip(with_spikes(result, jax.random.fold_in(rng, 3), *heavy), -most, most).astype(held_as)


def setup_inputs(seed: int = 0) -> dict:
    keys = jax.random.split(jax.random.key(seed), 8)
    return {
        "tokens": draw_tokens(jax.random.fold_in(keys[7], 71), 0),
        "norm_gain": jnp.clip(1.0 + 0.18 * jax.random.normal(keys[1], (D,), jnp.float32), 0.1, 1.9),
        "attend_weight": gaussian(keys[2], (3, D, D), D ** -0.5, 0.078125, ((1, 16), (2, 16))),
        "up_weight": gaussian(keys[3], (D, FF), D ** -0.5, 0.078125, ((0, 16), (1, 16))),
        "out_weight": gaussian(keys[4], (D, D), D ** -0.5, 0.078125, ((0, 16), (1, 16))),
        "down_weight": gaussian(keys[5], (FF, D), FF ** -0.5, 0.0390625, ((0, 16), (1, 16))),
        "upstream": heavy_noise(keys[6], (TOKENS, D), 1.0, 6.0, ((1, 16),), (1, 0, 16, 2.0)),
    }


EPS = 1e-06

def head_norm(values):
    count = values.shape[0]
    split = values.reshape(count, HEADS, HEAD_DIM)
    centred = split - lax.optimization_barrier(jnp.mean(split, -1, keepdims=True))
    scales = lax.rsqrt(lax.optimization_barrier(jnp.mean(centred * centred, -1, keepdims=True)) + EPS)
    return ((centred * scales).reshape(count, D), scales)

def norm_back(grads, normed, scales):
    count = grads.shape[0]
    upper = grads.reshape(count, HEADS, HEAD_DIM)
    shaped = normed.reshape(count, HEADS, HEAD_DIM)
    inner = upper - lax.optimization_barrier(jnp.mean(upper, -1, keepdims=True)) - shaped * lax.optimization_barrier(jnp.mean(upper * shaped, -1, keepdims=True))
    return (scales * inner).reshape(count, D)

def gelu_value(values):
    return 0.5 * values * (1.0 + jax.scipy.special.erf(values * 0.7071067811865476))

def gelu_slope(values):
    return 0.5 * (1.0 + jax.scipy.special.erf(values * 0.7071067811865476)) + values * jnp.exp(-0.5 * values * values) * 0.3989422804014327

def matmul(left, right):
    return jnp.dot(left, right, preferred_element_type=jnp.float32)

def reference(tokens, norm_gain, attend_weight, up_weight, out_weight, down_weight, upstream):
    inputs = tokens.astype(jnp.float32)
    row_mean = lax.optimization_barrier(jnp.mean(inputs, 1, keepdims=True))
    inv_scale = lax.rsqrt(lax.optimization_barrier(jnp.mean(inputs * inputs, 1, keepdims=True)) - row_mean * row_mean + EPS)
    centred = (inputs - row_mean) * inv_scale
    normed_rows = (centred * norm_gain[None, :]).astype(jnp.bfloat16)
    query_raw = matmul(normed_rows, attend_weight[0])
    key_raw = matmul(normed_rows, attend_weight[1])
    value_raw = matmul(normed_rows, attend_weight[2])
    up_raw = matmul(normed_rows, up_weight)
    query_normed, query_scales = head_norm(query_raw)
    key_normed, key_scales = head_norm(key_raw)
    shape_four = (IMG, SEQ, HEADS, HEAD_DIM)
    queries = query_normed.astype(jnp.bfloat16).reshape(shape_four).astype(jnp.float32)
    keys_all = key_normed.astype(jnp.bfloat16).reshape(shape_four).astype(jnp.float32)
    values_all = value_raw.astype(jnp.bfloat16).reshape(shape_four).astype(jnp.float32)
    score_scale = HEAD_DIM ** (-0.5)
    scores = jnp.einsum('bqhd,bkhd->bhqk', queries, keys_all) * score_scale
    weights = jnp.exp(scores)
    probabilities = weights / lax.optimization_barrier(jnp.sum(weights, -1, keepdims=True))
    probabilities_low = lax.optimization_barrier(probabilities.astype(jnp.bfloat16)).astype(jnp.float32)
    attended = jnp.einsum('bhqk,bkhd->bqhd', probabilities_low, values_all).reshape(TOKENS, D).astype(jnp.bfloat16)
    activated = gelu_value(up_raw).astype(jnp.bfloat16)
    branch = matmul(attended, out_weight) + matmul(activated, down_weight)
    layer_out = (inputs + branch).astype(jnp.bfloat16)
    out_grad = matmul(attended.T, upstream).astype(jnp.bfloat16)
    down_grad = matmul(activated.T, upstream).astype(jnp.bfloat16)
    attended_grad = matmul(upstream, out_weight.T).astype(jnp.bfloat16)
    activated_grad = matmul(upstream, down_weight.T).astype(jnp.bfloat16)
    up_grad_raw = activated_grad.astype(jnp.float32) * gelu_slope(up_raw)
    attended_four = attended_grad.reshape(shape_four).astype(jnp.float32)
    prob_grad = jnp.einsum('bqhd,bkhd->bhqk', attended_four, values_all)
    value_grad = jnp.einsum('bhqk,bqhd->bkhd', probabilities_low, attended_four).reshape(TOKENS, D)
    score_grad = probabilities * (prob_grad - lax.optimization_barrier(jnp.sum(prob_grad * probabilities, -1, keepdims=True))) * score_scale
    score_low = lax.optimization_barrier(score_grad.astype(jnp.bfloat16)).astype(jnp.float32)
    query_grad_n = jnp.einsum('bhqk,bkhd->bqhd', score_low, keys_all).reshape(TOKENS, D)
    key_grad_n = jnp.einsum('bhqk,bqhd->bkhd', score_low, queries).reshape(TOKENS, D)
    query_low = norm_back(query_grad_n, query_normed, query_scales).astype(jnp.bfloat16)
    key_low = norm_back(key_grad_n, key_normed, key_scales).astype(jnp.bfloat16)
    value_low = value_grad.astype(jnp.bfloat16)
    up_low = up_grad_raw.astype(jnp.bfloat16)
    normed_t = normed_rows.T
    attend_grad = jnp.stack([matmul(normed_t, query_low), matmul(normed_t, key_low), matmul(normed_t, value_low)]).astype(jnp.bfloat16)
    up_grad = matmul(normed_t, up_low).astype(jnp.bfloat16)
    normed_grad = matmul(query_low, attend_weight[0].T) + matmul(key_low, attend_weight[1].T)
    normed_grad = normed_grad + matmul(value_low, attend_weight[2].T) + matmul(up_low, up_weight.T)
    gain_grad = lax.optimization_barrier(jnp.sum(normed_grad * centred, 0))
    scaled_grad = normed_grad * norm_gain[None, :]
    inner = scaled_grad - lax.optimization_barrier(jnp.mean(scaled_grad, 1, keepdims=True)) - centred * lax.optimization_barrier(jnp.mean(scaled_grad * centred, 1, keepdims=True))
    tokens_grad = (upstream.astype(jnp.float32) + inv_scale * inner).astype(jnp.bfloat16)
    return (layer_out, tokens_grad, gain_grad, attend_grad, up_grad, out_grad, down_grad)
```

```python
import jax
import jax.numpy as jnp
from jax import lax
from jax.experimental import pallas as pl
from jax.experimental.pallas import tpu as pltpu
from jax.sharding import PartitionSpec as P

D = 6144
HEAD_DIM = 128
T = 256
W = 384
FF = 1536
EPS = 1e-06
BF = jnp.bfloat16
F32 = jnp.float32
MESH = pl.DeviceIdType.MESH
HIGH = lax.Precision.HIGHEST

ACT1 = 1024
ACT2 = FF - ACT1
UP1 = 768
UP2 = FF - UP1
CHUNKS = {"c0": W + ACT1, "c1": 3 * W, "c2": UP1, "c3": UP2, "c4": ACT2}
GROUPS = {"a0": 4 * W, "a1": UP1, "a2": UP2, "a3": ACT1, "a4": ACT2}


def scratch_shapes():
    shapes = {
        "tok": ((T, W), BF),
        "gain": ((1, W), F32),
        "aw": ((3, W, W), BF),
        "uw": ((W, FF), BF),
        "ow": ((W, W), BF),
        "dw": ((FF, W), BF),
        "ups": ((T, W), BF),
        "stz": ((4, 8, T), F32),
        "sty": ((4, 8, T), F32),
        "nr": ((T, W), BF),
        "nrt": ((W, T), BF),
        "cen": ((T, W), F32),
        "inv": ((T, 128), F32),
        "rawup": ((16, FF), F32),
        "actg": ((16, FF), F32),
        "attg": ((16, W), BF),
        "att": ((T, W), BF),
        "low": ((3, T, W), BF),
        "ng": ((T, W), F32),
        "og_v": ((W, W), BF),
        "dg_v": ((FF, W), BF),
        "ag_v": ((3, W, W), BF),
        "ug_v": ((W, FF), BF),
        "lo_v": ((T, W), BF),
        "tg_v": ((T, W), BF),
        "gg_v": ((1, W), F32),
        "fsy": ((4, 8, T), F32),
        "fsz": ((4, 8, T), F32),
        "fsc": ((2, 8, T), F32),
        "fsx": ((4, 8, T), F32),
        "fsh": ((2, 8, T), F32),
    }
    for name, w in CHUNKS.items():
        shapes[name + "P"] = ((T, w), BF)
        shapes[name + "R1"] = ((2, 32, w), BF)
        shapes[name + "R2"] = ((2, 64, w), BF)
        shapes[name + "T"] = ((2, 32, w), BF)
        shapes[name + "S"] = ((64, w), BF)
        shapes[name + "Z"] = ((3, 16, w), BF)
    for name, w in GROUPS.items():
        shapes[name + "G"] = ((T, w), BF)
    for name in ("b", "n"):
        shapes[name + "Q"] = ((T, W), BF)
        shapes[name + "AC"] = ((128, W), BF)
        shapes[name + "H1"] = ((128, W), BF)
        shapes[name + "AX"] = ((3, 32, W), BF)
        shapes[name + "H2"] = ((32, W), BF)
        shapes[name + "AZ"] = ((32, W), BF)
        shapes[name + "R"] = ((T, W), BF)
    return shapes


SHAPES = scratch_shapes()
N_COPIES = 140


def nt(a, b, **kw):
    return lax.dot_general(a, b, (((1,), (1,)), ((), ())), preferred_element_type=F32, **kw)


def tn(a, b):
    return lax.dot_general(a, b, (((0,), (0,)), ((), ())), preferred_element_type=F32)


def nn(a, b):
    return jnp.dot(a, b, preferred_element_type=F32)


def rows(start, size):
    return pl.ds(pl.multiple_of(start, 16), size)


def kernel(tok_h, gain_h, aw_h, uw_h, ow_h, dw_h, ups_h, lo_h, tg_h, gg_h, ag_out, ug_h, og_h, dg_h, *scr):
    s = dict(zip(SHAPES, scr[: len(SHAPES)]))
    send_sem, recv_sem, load_sem, store_sem = scr[len(SHAPES) :]

    f = lax.axis_index("fin")
    g = lax.axis_index("fout")
    y, z = f // 4, f % 4
    x, h, c = g // 4, (g // 2) % 2, g % 2

    def fin_dev(yy, zz):
        return (yy * 4 + zz, g)

    def fout_dev(xx, hh, cc):
        return (f, xx * 4 + hh * 2 + cc)

    right, left = lax.rem(y + 1, 4), lax.rem(y + 3, 4)
    far = lax.rem(y + 2, 4)
    dev_right, dev_left = fin_dev(right, z), fin_dev(left, z)
    y_devs = [fin_dev(lax.rem(y + d, 4), z) for d in (1, 2, 3)]
    z_devs = [fin_dev(y, lax.rem(z + d, 4)) for d in (1, 2, 3)]
    x_devs = [fout_dev(lax.rem(x + d, 4), h, c) for d in (1, 2, 3)]
    h_dev = fout_dev(x, 1 - h, c)
    c_dev = fout_dev(x, h, 1 - c)
    peers = y_devs + z_devs + x_devs + [h_dev, c_dev]

    loads = {}
    for i, (name, src) in enumerate(
        [("tok", tok_h), ("ups", ups_h), ("ow", ow_h), ("dw", dw_h), ("gain", gain_h), ("aw", aw_h), ("uw", uw_h)]
    ):
        loads[name] = pltpu.make_async_copy(src, s[name], load_sem.at[i])
        loads[name].start()

    barrier = pltpu.get_barrier_semaphore()
    for dev in peers:
        pl.semaphore_signal(barrier, inc=1, device_id=dev, device_id_type=MESH)

    copies = []
    stores = []

    def rcopy(src, dst, dev):
        i = len(copies)
        cp = pltpu.make_async_remote_copy(
            src_ref=src,
            dst_ref=dst,
            send_sem=send_sem.at[i],
            recv_sem=recv_sem.at[i],
            device_id=dev,
            device_id_type=MESH,
        )
        cp.start()
        copies.append(cp)
        return cp

    def store(src, dst):
        cp = pltpu.make_async_copy(src, dst, store_sem.at[len(stores)])
        cp.start()
        stores.append(cp)

    pending = {}

    def rs_a(n):
        p, r1, r2 = s[n + "P"], s[n + "R1"], s[n + "R2"]
        pending[n + "r1"] = [
            rcopy(p.at[rows(far * 64, 32)], r1.at[0], dev_right),
            rcopy(p.at[rows(far * 64 + 32, 32)], r1.at[1], dev_left),
        ]
        pending[n + "r2"] = [
            rcopy(p.at[rows(right * 64 + 32, 32)], r2.at[0, pl.ds(32, 32)], dev_right),
            rcopy(p.at[rows(left * 64, 32)], r2.at[1, pl.ds(0, 32)], dev_left),
        ]

    def rs_b(n):
        p, r1, r2, t = s[n + "P"], s[n + "R1"], s[n + "R2"], s[n + "T"]
        first, second = pending[n + "r1"]
        first.wait_recv()
        t[0] = (p[rows(right * 64, 32)].astype(F32) + r1[0].astype(F32)).astype(BF)
        pending[n + "r2"].append(rcopy(t.at[0], r2.at[0, pl.ds(0, 32)], dev_right))
        second.wait_recv()
        t[1] = (p[rows(left * 64 + 32, 32)].astype(F32) + r1[1].astype(F32)).astype(BF)
        pending[n + "r2"].append(rcopy(t.at[1], r2.at[1, pl.ds(32, 32)], dev_left))

    def rs_c(n):
        p, r2, sm, zz = s[n + "P"], s[n + "R2"], s[n + "S"], s[n + "Z"]
        for cp in pending[n + "r2"]:
            cp.wait_recv()
        sm[...] = (p[rows(y * 64, 64)].astype(F32) + r2[0].astype(F32) + r2[1].astype(F32)).astype(BF)
        pending[n + "z"] = [
            rcopy(sm.at[rows(lax.rem(z + d, 4) * 16, 16)], zz.at[d - 1], z_devs[d - 1]) for d in (1, 2, 3)
        ]

    def rs_d(n):
        sm, zz = s[n + "S"], s[n + "Z"]
        for cp in pending[n + "z"]:
            cp.wait_recv()
        return (
            sm[rows(z * 16, 16)].astype(F32) + zz[0].astype(F32) + zz[1].astype(F32) + zz[2].astype(F32)
        )

    def ag_e(n):
        gr = s[n + "G"]
        own = gr.at[rows(f * 16, 16)]
        pending[n + "e"] = [rcopy(own, own, dev) for dev in z_devs]

    def ag_f(n):
        gr = s[n + "G"]
        for cp in pending[n + "e"]:
            cp.wait_recv()
        block = gr.at[rows(y * 64, 64)]
        pending[n + "f"] = [rcopy(block, block, dev_right), rcopy(block, block, dev_left)]

    def ag_h(n):
        gr = s[n + "G"]
        first, second = pending[n + "f"]
        first.wait_recv()
        one = gr.at[rows(left * 64, 32)]
        cps = [rcopy(one, one, dev_right)]
        second.wait_recv()
        two = gr.at[rows(right * 64 + 32, 32)]
        cps.append(rcopy(two, two, dev_left))
        pending[n + "h"] = cps

    def ag_i(n):
        for cp in pending[n + "h"]:
            cp.wait_recv()

    def ar_1(n):
        q = s[n + "Q"]
        pending[n + "1"] = rcopy(q.at[rows((1 - c) * 128, 128)], s[n + "AC"], c_dev)

    def ar_2(n):
        q, h1, ax = s[n + "Q"], s[n + "H1"], s[n + "AX"]
        pending[n + "1"].wait_recv()
        h1[...] = (q[rows(c * 128, 128)].astype(F32) + s[n + "AC"][...].astype(F32)).astype(BF)
        pending[n + "2"] = [
            rcopy(h1.at[rows(lax.rem(x + d, 4) * 32, 32)], ax.at[d - 1], x_devs[d - 1]) for d in (1, 2, 3)
        ]

    def ar_3(n):
        h1, ax, h2 = s[n + "H1"], s[n + "AX"], s[n + "H2"]
        for cp in pending[n + "2"]:
            cp.wait_recv()
        h2[...] = (
            h1[rows(x * 32, 32)].astype(F32) + ax[0].astype(F32) + ax[1].astype(F32) + ax[2].astype(F32)
        ).astype(BF)
        pending[n + "3"] = rcopy(h2, s[n + "AZ"], h_dev)

    def ar_4(n):
        res = s[n + "R"]
        pending[n + "3"].wait_recv()
        at = rows(c * 128 + x * 32, 32)
        res[at] = (s[n + "H2"][...].astype(F32) + s[n + "AZ"][...].astype(F32)).astype(BF)
        pending[n + "4"] = [rcopy(res.at[at], res.at[at], dev) for dev in x_devs]

    def ar_5(n):
        res = s[n + "R"]
        for cp in pending[n + "4"]:
            cp.wait_recv()
        at = res.at[rows(c * 128, 128)]
        pending[n + "5"] = rcopy(at, at, c_dev)

    def ar_6(n):
        pending[n + "5"].wait_recv()
        return s[n + "R"][...].astype(F32)

    def ex_start(buf, value, slot, devs):
        buf[slot] = value
        return [rcopy(buf.at[slot], buf.at[slot], dev) for dev in devs]

    def ex_sum(buf, cps):
        for cp in cps:
            cp.wait_recv()
        return sum(buf[i] for i in range(1, buf.shape[0])) + buf[0]

    row_id = lax.broadcasted_iota(jnp.int32, (8, W), 0)
    pick0 = jnp.where(row_id == 0, 1.0, 0.0).astype(F32)
    pick1 = jnp.where(row_id == 1, 1.0, 0.0).astype(F32)

    def pair_sums(first, second):
        return nt(pick0, first, precision=HIGH) + nt(pick1, second, precision=HIGH)

    loads["tok"].wait()
    inputs = s["tok"][...].astype(F32)
    stats = pair_sums(inputs, inputs * inputs)
    loads["ups"].wait()
    loads["ow"].wait()
    loads["dw"].wait()
    pl.semaphore_wait(barrier, len(peers))
    st_cps = ex_start(s["stz"], stats, z, z_devs)

    ups = s["ups"][...]
    s["c0P"][:, 0:W] = nt(ups, s["ow"][...]).astype(BF)
    for i in range(0, ACT1, 512):
        s["c0P"][:, W + i : W + i + 512] = nt(ups, s["dw"][i : i + 512, :]).astype(BF)
    rs_a("c0")
    stats = ex_sum(s["stz"], st_cps)
    st_cps = ex_start(s["sty"], stats, y, y_devs)
    s["c4P"][...] = nt(ups, s["dw"][ACT1:FF, :]).astype(BF)
    rs_b("c0")
    stats = ex_sum(s["sty"], st_cps)
    columns = jnp.concatenate([stats] * 16, 0).T
    row_mean = columns[:, 0:1] / D
    inv_scale = lax.rsqrt(columns[:, 1:2] / D - row_mean * row_mean + EPS)
    centred = (inputs - row_mean) * inv_scale
    s["cen"][...] = centred
    s["inv"][...] = jnp.broadcast_to(inv_scale, (T, 128))
    loads["gain"].wait()
    normed = (centred * s["gain"][...]).astype(BF)
    s["nr"][...] = normed
    loads["aw"].wait()
    for i in range(3):
        s["c1P"][:, i * W : (i + 1) * W] = nn(normed, s["aw"][i]).astype(BF)
    rs_a("c1")
    loads["uw"].wait()
    for i in range(0, UP1, 384):
        s["c2P"][:, i : i + 384] = nn(normed, s["uw"][:, i : i + 384]).astype(BF)
    rs_a("c2")
    rs_c("c0")
    rs_b("c1")
    for i in range(0, UP2, 384):
        s["c3P"][:, i : i + 384] = nn(normed, s["uw"][:, UP1 + i : UP1 + i + 384]).astype(BF)
    rs_a("c3")
    rs_a("c4")
    rs_b("c2")
    rs_c("c1")
    part = rs_d("c0")
    s["attg"][...] = part[:, 0:W].astype(BF)
    s["actg"][:, 0:ACT1] = part[:, W:].astype(BF).astype(F32)
    rs_b("c3")
    rs_c("c2")
    own = rows(f * 16, 16)
    s["a0G"][own, 0 : 3 * W] = rs_d("c1").astype(BF)
    s["a0G"][own, 3 * W : 4 * W] = s["attg"][...]
    ag_e("a0")
    rs_b("c4")
    rs_c("c3")

    def gelu_value(v):
        return 0.5 * v * (1.0 + lax.erf(v * 0.7071067811865476))

    def gelu_slope(v):
        return (
            0.5 * (1.0 + lax.erf(v * 0.7071067811865476)) + v * jnp.exp(-0.5 * v * v) * 0.3989422804014327
        )

    part = rs_d("c2")
    s["rawup"][:, 0:UP1] = part
    s["a1G"][own, :] = gelu_value(part).astype(BF)
    ag_e("a1")
    ag_f("a0")
    rs_c("c4")
    part = rs_d("c3")
    s["rawup"][:, UP1:FF] = part
    s["a2G"][own, :] = gelu_value(part).astype(BF)
    ag_e("a2")
    s["a3G"][own, :] = (s["actg"][:, 0:ACT1] * gelu_slope(s["rawup"][:, 0:ACT1])).astype(BF)
    ag_e("a3")
    ag_f("a1")
    part = rs_d("c4").astype(BF).astype(F32)
    s["a4G"][own, :] = (part * gelu_slope(s["rawup"][:, ACT1:FF])).astype(BF)
    ag_e("a4")
    ag_h("a0")
    ag_f("a2")
    ag_h("a1")
    ag_f("a3")
    ag_i("a0")

    score_scale = HEAD_DIM ** (-0.5)

    def head_norm(v):
        cent = v - jnp.mean(v, -1, keepdims=True)
        scale = lax.rsqrt(jnp.mean(cent * cent, -1, keepdims=True) + EPS)
        return cent * scale, scale

    def norm_back(gr, normed_v, scale):
        return scale * (
            gr - jnp.mean(gr, -1, keepdims=True) - normed_v * jnp.mean(gr * normed_v, -1, keepdims=True)
        )

    def head(i):
        lo = i * HEAD_DIM
        hi = lo + HEAD_DIM
        gr = s["a0G"]
        qn, qs = head_norm(gr[:, lo:hi].astype(F32))
        kn, ks = head_norm(gr[:, W + lo : W + hi].astype(F32))
        v = gr[:, 2 * W + lo : 2 * W + hi]
        da = gr[:, 3 * W + lo : 3 * W + hi]
        q, k = qn.astype(BF), kn.astype(BF)
        e = jnp.exp(nt(q, k) * score_scale)
        p = e / jnp.sum(e, -1, keepdims=True)
        pl_ = p.astype(BF)
        s["att"][:, lo:hi] = nn(pl_, v).astype(BF)
        dp = nt(da, v)
        ds = (p * (dp - jnp.sum(dp * p, -1, keepdims=True)) * score_scale).astype(BF)
        s["low"][0, :, lo:hi] = norm_back(nn(ds, k), qn, qs).astype(BF)
        s["low"][1, :, lo:hi] = norm_back(tn(ds, q), kn, ks).astype(BF)
        s["low"][2, :, lo:hi] = tn(pl_, da).astype(BF)

    head(0)
    ag_h("a2")
    ag_f("a4")
    head(1)
    ag_h("a3")
    head(2)
    ag_i("a1")
    ag_i("a2")
    branch = nn(s["att"][...], s["ow"][...])
    branch += nn(s["a1G"][...], s["dw"][0:UP1, :])
    branch += nn(s["a2G"][...], s["dw"][UP1:FF, :])
    s["bQ"][...] = branch.astype(BF)
    ar_1("b")
    ag_h("a4")
    ngrad = nt(s["low"][0], s["aw"][0]) + nt(s["low"][1], s["aw"][1]) + nt(s["low"][2], s["aw"][2])
    s["ng"][...] = ngrad
    ar_2("b")
    s["nrt"][...] = s["nr"][...].T
    for i in range(3):
        s["ag_v"][i] = nn(s["nrt"][...], s["low"][i]).astype(BF)
    store(s["ag_v"], ag_out)
    ar_3("b")
    ag_i("a3")
    ngrad = s["ng"][...] + nt(s["a3G"][...], s["uw"][:, 0:ACT1])
    ag_i("a4")
    ngrad = ngrad + nt(s["a4G"][...], s["uw"][:, ACT1:FF])
    s["nQ"][...] = ngrad.astype(BF)
    ar_1("n")
    scaled = ngrad * s["gain"][...]
    sums = pair_sums(scaled, scaled * s["cen"][...])
    sm_cps = ex_start(s["fsy"], sums, y, y_devs)
    ar_2("n")
    s["og_v"][...] = tn(s["att"][...], ups).astype(BF)
    store(s["og_v"], og_h)
    for i in range(0, ACT1, 512):
        s["ug_v"][:, i : i + 512] = nn(s["nrt"][...], s["a3G"][:, i : i + 512]).astype(BF)
    ar_4("b")
    sums = ex_sum(s["fsy"], sm_cps)
    sm_cps = ex_start(s["fsz"], sums, z, z_devs)
    ar_3("n")
    s["ug_v"][:, ACT1:FF] = nn(s["nrt"][...], s["a4G"][...]).astype(BF)
    store(s["ug_v"], ug_h)
    sums = ex_sum(s["fsz"], sm_cps)
    sm_cps = ex_start(s["fsc"], sums, c, [c_dev])
    for i in range(0, UP1, 384):
        s["dg_v"][i : i + 384, :] = tn(s["a1G"][:, i : i + 384], ups).astype(BF)
    sums = ex_sum(s["fsc"], sm_cps)
    sm_cps = ex_start(s["fsx"], sums, x, x_devs)
    ar_4("n")
    ar_5("b")
    for i in range(0, UP2, 384):
        s["dg_v"][UP1 + i : UP1 + i + 384, :] = tn(s["a2G"][:, i : i + 384], ups).astype(BF)
    store(s["dg_v"], dg_h)
    sums = ex_sum(s["fsx"], sm_cps)
    sm_cps = ex_start(s["fsh"], sums, h, [h_dev])
    ar_5("n")
    s["lo_v"][...] = (s["tok"][...].astype(F32) + ar_6("b")).astype(BF)
    store(s["lo_v"], lo_h)
    sums = ex_sum(s["fsh"], sm_cps)
    columns = jnp.concatenate([sums] * 16, 0).T
    grad_mean = columns[:, 0:1] / D
    grad_cross = columns[:, 1:2] / D
    ngrad = ar_6("n")
    centred = s["cen"][...]
    s["gg_v"][...] = jnp.sum(ngrad * centred, 0, keepdims=True)
    store(s["gg_v"], gg_h)
    inner = ngrad * s["gain"][...] - grad_mean - centred * grad_cross
    s["tg_v"][...] = (ups.astype(F32) + s["inv"][:, 0:1] * inner).astype(BF)
    store(s["tg_v"], tg_h)

    for cp in copies:
        cp.wait_send()
    for cp in stores:
        cp.wait()


def body(tokens, norm_gain, attend_weight, up_weight, out_weight, down_weight, upstream):
    any_spec = pl.BlockSpec(memory_space=pl.ANY)
    outs = pl.pallas_call(
        kernel,
        out_shape=(
            jax.ShapeDtypeStruct((T, W), BF),
            jax.ShapeDtypeStruct((T, W), BF),
            jax.ShapeDtypeStruct((1, W), F32),
            jax.ShapeDtypeStruct((3, W, W), BF),
            jax.ShapeDtypeStruct((W, FF), BF),
            jax.ShapeDtypeStruct((W, W), BF),
            jax.ShapeDtypeStruct((FF, W), BF),
        ),
        in_specs=[any_spec] * 7,
        out_specs=(any_spec,) * 7,
        scratch_shapes=[pltpu.VMEM(shape, dtype) for shape, dtype in SHAPES.values()]
        + [
            pltpu.SemaphoreType.DMA((N_COPIES,)),
            pltpu.SemaphoreType.DMA((N_COPIES,)),
            pltpu.SemaphoreType.DMA((8,)),
            pltpu.SemaphoreType.DMA((8,)),
        ],
        compiler_params=pltpu.CompilerParams(
            collective_id=0, has_side_effects=True, vmem_limit_bytes=56 * 1024 * 1024
        ),
        name="layer",
    )(tokens, norm_gain.reshape(1, W), attend_weight, up_weight, out_weight, down_weight, upstream)
    layer_out, tokens_grad, gain_grad, attend_grad, up_grad, out_grad, down_grad = outs
    return (layer_out, tokens_grad, gain_grad.reshape(W), attend_grad, up_grad, out_grad, down_grad)


def solution(mesh):
    return jax.shard_map(
        body,
        mesh=mesh,
        in_specs=(
            P(None, "fin"),
            P("fin"),
            P(None, "fin", "fout"),
            P("fin", "fout"),
            P("fout", "fin"),
            P("fout", "fin"),
            P(None, "fin"),
        ),
        out_specs=(
            P(None, "fin"),
            P(None, "fin"),
            P("fin"),
            P(None, "fin", "fout"),
            P("fin", "fout"),
            P("fout", "fin"),
            P("fout", "fin"),
        ),
        check_vma=False,
    )
```

```python
import jax
import jax.numpy as jnp
from jax import lax
from jax.experimental import pallas as pl
from jax.experimental.pallas import tpu as pltpu
from jax.sharding import PartitionSpec as P

D = 6144
HEAD_DIM = 128
T = 256
W = 384
FF = 1536
EPS = 1e-06
BF = jnp.bfloat16
F32 = jnp.float32
MESH = pl.DeviceIdType.MESH
HIGH = lax.Precision.HIGHEST

ACT1 = 1024
ACT2 = FF - ACT1
UP1 = 768
UP2 = FF - UP1
CHUNKS = {"c0": W + ACT1, "c1": 3 * W, "c2": UP1, "c3": UP2, "c4": ACT2}
GROUPS = {"a0": 4 * W, "a1": UP1, "a2": UP2, "a3": ACT1, "a4": ACT2}


def scratch_shapes():
    shapes = {
        "tok": ((T, W), BF),
        "gain": ((W,), F32),
        "aw": ((3, W, W), BF),
        "uw": ((W, FF), BF),
        "ow": ((W, W), BF),
        "dw": ((FF, W), BF),
        "ups": ((T, W), BF),
        "stz": ((4, 8, T), F32),
        "sty": ((4, 8, T), F32),
        "nr": ((T, W), BF),
        "nrt": ((W, T), BF),
        "cen": ((T, W), F32),
        "inv": ((T, 128), F32),
        "rawup": ((16, FF), F32),
        "actg": ((16, FF), F32),
        "attg": ((16, W), BF),
        "att": ((T, W), BF),
        "low": ((3, T, W), BF),
        "ng": ((T, W), F32),
        "fsy": ((4, 8, T), F32),
        "fsz": ((4, 8, T), F32),
        "fsc": ((2, 8, T), F32),
        "fsx": ((4, 8, T), F32),
        "fsh": ((2, 8, T), F32),
    }
    for name, w in CHUNKS.items():
        shapes[name + "P"] = ((T, w), BF)
        shapes[name + "R1"] = ((2, 32, w), BF)
        shapes[name + "R2"] = ((2, 64, w), BF)
        shapes[name + "T"] = ((2, 32, w), BF)
        shapes[name + "S"] = ((64, w), BF)
        shapes[name + "Z"] = ((3, 16, w), BF)
    for name, w in GROUPS.items():
        shapes[name + "G"] = ((T, w), BF)
    for name in ("b", "n"):
        shapes[name + "Q"] = ((T, W), BF)
        shapes[name + "AC"] = ((128, W), BF)
        shapes[name + "H1"] = ((128, W), BF)
        shapes[name + "AX"] = ((3, 32, W), BF)
        shapes[name + "H2"] = ((32, W), BF)
        shapes[name + "AZ"] = ((32, W), BF)
        shapes[name + "R"] = ((T, W), BF)
    return shapes


SHAPES = scratch_shapes()
N_COPIES = 140


def nt(a, b, **kw):
    return lax.dot_general(a, b, (((1,), (1,)), ((), ())), preferred_element_type=F32, **kw)


def tn(a, b):
    return lax.dot_general(a, b, (((0,), (0,)), ((), ())), preferred_element_type=F32)


def nn(a, b):
    return jnp.dot(a, b, preferred_element_type=F32)


def rows(start, size):
    return pl.ds(pl.multiple_of(start, 16), size)


def kernel(tok_h, gain_h, aw_h, uw_h, ow_h, dw_h, ups_h, *refs):
    outs, scr = refs[:7], refs[7:]
    s = dict(zip(SHAPES, scr[: len(SHAPES)]))
    s.update(zip(("lo_v", "tg_v", "gg_v", "ag_v", "ug_v", "og_v", "dg_v"), outs))
    send_sem, recv_sem, load_sem = scr[len(SHAPES) :]

    f = lax.axis_index("fin")
    g = lax.axis_index("fout")
    y, z = f // 4, f % 4
    x, h, c = g // 4, (g // 2) % 2, g % 2

    def fin_dev(yy, zz):
        return (yy * 4 + zz, g)

    def fout_dev(xx, hh, cc):
        return (f, xx * 4 + hh * 2 + cc)

    right, left = lax.rem(y + 1, 4), lax.rem(y + 3, 4)
    far = lax.rem(y + 2, 4)
    dev_right, dev_left = fin_dev(right, z), fin_dev(left, z)
    y_devs = [fin_dev(lax.rem(y + d, 4), z) for d in (1, 2, 3)]
    z_devs = [fin_dev(y, lax.rem(z + d, 4)) for d in (1, 2, 3)]
    x_devs = [fout_dev(lax.rem(x + d, 4), h, c) for d in (1, 2, 3)]
    h_dev = fout_dev(x, 1 - h, c)
    c_dev = fout_dev(x, h, 1 - c)
    peers = y_devs + z_devs + x_devs + [h_dev, c_dev]

    loads = {}
    for i, (name, src) in enumerate(
        [("tok", tok_h), ("ups", ups_h), ("ow", ow_h), ("dw", dw_h), ("gain", gain_h), ("aw", aw_h), ("uw", uw_h)]
    ):
        loads[name] = pltpu.make_async_copy(src, s[name], load_sem.at[i])
        loads[name].start()

    barrier = pltpu.get_barrier_semaphore()
    for dev in peers:
        pl.semaphore_signal(barrier, inc=1, device_id=dev, device_id_type=MESH)

    copies = []

    def rcopy(src, dst, dev):
        i = len(copies)
        cp = pltpu.make_async_remote_copy(
            src_ref=src,
            dst_ref=dst,
            send_sem=send_sem.at[i],
            recv_sem=recv_sem.at[i],
            device_id=dev,
            device_id_type=MESH,
        )
        cp.start()
        copies.append(cp)
        return cp

    pending = {}

    def rs_a(n):
        p, r1, r2 = s[n + "P"], s[n + "R1"], s[n + "R2"]
        pending[n + "r1"] = [
            rcopy(p.at[rows(far * 64, 32)], r1.at[0], dev_right),
            rcopy(p.at[rows(far * 64 + 32, 32)], r1.at[1], dev_left),
        ]
        pending[n + "r2"] = [
            rcopy(p.at[rows(right * 64 + 32, 32)], r2.at[0, pl.ds(32, 32)], dev_right),
            rcopy(p.at[rows(left * 64, 32)], r2.at[1, pl.ds(0, 32)], dev_left),
        ]

    def rs_b(n):
        p, r1, r2, t = s[n + "P"], s[n + "R1"], s[n + "R2"], s[n + "T"]
        first, second = pending[n + "r1"]
        first.wait_recv()
        t[0] = (p[rows(right * 64, 32)].astype(F32) + r1[0].astype(F32)).astype(BF)
        pending[n + "r2"].append(rcopy(t.at[0], r2.at[0, pl.ds(0, 32)], dev_right))
        second.wait_recv()
        t[1] = (p[rows(left * 64 + 32, 32)].astype(F32) + r1[1].astype(F32)).astype(BF)
        pending[n + "r2"].append(rcopy(t.at[1], r2.at[1, pl.ds(32, 32)], dev_left))

    def rs_c(n):
        p, r2, sm, zz = s[n + "P"], s[n + "R2"], s[n + "S"], s[n + "Z"]
        for cp in pending[n + "r2"]:
            cp.wait_recv()
        sm[...] = (p[rows(y * 64, 64)].astype(F32) + r2[0].astype(F32) + r2[1].astype(F32)).astype(BF)
        pending[n + "z"] = [
            rcopy(sm.at[rows(lax.rem(z + d, 4) * 16, 16)], zz.at[d - 1], z_devs[d - 1]) for d in (1, 2, 3)
        ]

    def rs_d(n):
        sm, zz = s[n + "S"], s[n + "Z"]
        for cp in pending[n + "z"]:
            cp.wait_recv()
        return (
            sm[rows(z * 16, 16)].astype(F32) + zz[0].astype(F32) + zz[1].astype(F32) + zz[2].astype(F32)
        )

    def ag_e(n):
        gr = s[n + "G"]
        own = gr.at[rows(f * 16, 16)]
        pending[n + "e"] = [rcopy(own, own, dev) for dev in z_devs]

    def ag_f(n):
        gr = s[n + "G"]
        for cp in pending[n + "e"]:
            cp.wait_recv()
        block = gr.at[rows(y * 64, 64)]
        pending[n + "f"] = [rcopy(block, block, dev_right), rcopy(block, block, dev_left)]

    def ag_h(n):
        gr = s[n + "G"]
        first, second = pending[n + "f"]
        first.wait_recv()
        one = gr.at[rows(left * 64, 32)]
        cps = [rcopy(one, one, dev_right)]
        second.wait_recv()
        two = gr.at[rows(right * 64 + 32, 32)]
        cps.append(rcopy(two, two, dev_left))
        pending[n + "h"] = cps

    def ag_i(n):
        for cp in pending[n + "h"]:
            cp.wait_recv()

    def ar_1(n):
        q = s[n + "Q"]
        pending[n + "1"] = rcopy(q.at[rows((1 - c) * 128, 128)], s[n + "AC"], c_dev)

    def ar_2(n):
        q, h1, ax = s[n + "Q"], s[n + "H1"], s[n + "AX"]
        pending[n + "1"].wait_recv()
        h1[...] = (q[rows(c * 128, 128)].astype(F32) + s[n + "AC"][...].astype(F32)).astype(BF)
        pending[n + "2"] = [
            rcopy(h1.at[rows(lax.rem(x + d, 4) * 32, 32)], ax.at[d - 1], x_devs[d - 1]) for d in (1, 2, 3)
        ]

    def ar_3(n):
        h1, ax, h2 = s[n + "H1"], s[n + "AX"], s[n + "H2"]
        for cp in pending[n + "2"]:
            cp.wait_recv()
        h2[...] = (
            h1[rows(x * 32, 32)].astype(F32) + ax[0].astype(F32) + ax[1].astype(F32) + ax[2].astype(F32)
        ).astype(BF)
        pending[n + "3"] = rcopy(h2, s[n + "AZ"], h_dev)

    def ar_4(n):
        res = s[n + "R"]
        pending[n + "3"].wait_recv()
        at = rows(c * 128 + x * 32, 32)
        res[at] = (s[n + "H2"][...].astype(F32) + s[n + "AZ"][...].astype(F32)).astype(BF)
        pending[n + "4"] = [rcopy(res.at[at], res.at[at], dev) for dev in x_devs]

    def ar_5(n):
        res = s[n + "R"]
        for cp in pending[n + "4"]:
            cp.wait_recv()
        at = res.at[rows(c * 128, 128)]
        pending[n + "5"] = rcopy(at, at, c_dev)

    def ar_6(n):
        pending[n + "5"].wait_recv()
        return s[n + "R"][...].astype(F32)

    def ex_start(buf, value, slot, devs):
        buf[slot] = value
        return [rcopy(buf.at[slot], buf.at[slot], dev) for dev in devs]

    def ex_sum(buf, cps):
        for cp in cps:
            cp.wait_recv()
        return sum(buf[i] for i in range(1, buf.shape[0])) + buf[0]

    row_id = lax.broadcasted_iota(jnp.int32, (8, W), 0)
    pick0 = jnp.where(row_id == 0, 1.0, 0.0).astype(F32)
    pick1 = jnp.where(row_id == 1, 1.0, 0.0).astype(F32)

    def pair_sums(first, second):
        return nt(pick0, first, precision=HIGH) + nt(pick1, second, precision=HIGH)

    loads["tok"].wait()
    inputs = s["tok"][...].astype(F32)
    stats = pair_sums(inputs, inputs * inputs)

    loads["ups"].wait()
    loads["ow"].wait()
    loads["dw"].wait()
    ups = s["ups"][...]
    s["c0P"][:, 0:W] = nt(ups, s["ow"][...]).astype(BF)
    for i in range(0, ACT1, 512):
        s["c0P"][:, W + i : W + i + 512] = nt(ups, s["dw"][i : i + 512, :]).astype(BF)
    s["c4P"][...] = nt(ups, s["dw"][ACT1:FF, :]).astype(BF)
    pl.semaphore_wait(barrier, len(peers))
    st_cps = ex_start(s["stz"], stats, z, z_devs)
    rs_a("c0")
    stats = ex_sum(s["stz"], st_cps)
    st_cps = ex_start(s["sty"], stats, y, y_devs)
    rs_b("c0")
    stats = ex_sum(s["sty"], st_cps)
    columns = jnp.concatenate([stats] * 16, 0).T
    row_mean = columns[:, 0:1] / D
    inv_scale = lax.rsqrt(columns[:, 1:2] / D - row_mean * row_mean + EPS)
    centred = (inputs - row_mean) * inv_scale
    s["cen"][...] = centred
    s["inv"][...] = jnp.broadcast_to(inv_scale, (T, 128))
    loads["gain"].wait()
    normed = (centred * s["gain"][...][None, :]).astype(BF)
    s["nr"][...] = normed
    loads["aw"].wait()
    for i in range(3):
        s["c1P"][:, i * W : (i + 1) * W] = nn(normed, s["aw"][i]).astype(BF)
    rs_a("c1")
    loads["uw"].wait()
    for i in range(0, UP1, 384):
        s["c2P"][:, i : i + 384] = nn(normed, s["uw"][:, i : i + 384]).astype(BF)
    rs_a("c2")
    rs_c("c0")
    rs_b("c1")
    for i in range(0, UP2, 384):
        s["c3P"][:, i : i + 384] = nn(normed, s["uw"][:, UP1 + i : UP1 + i + 384]).astype(BF)
    rs_a("c3")
    rs_a("c4")
    rs_b("c2")
    rs_c("c1")
    part = rs_d("c0")
    s["attg"][...] = part[:, 0:W].astype(BF)
    s["actg"][:, 0:ACT1] = part[:, W:].astype(BF).astype(F32)
    rs_b("c3")
    rs_c("c2")
    own = rows(f * 16, 16)
    s["a0G"][own, 0 : 3 * W] = rs_d("c1").astype(BF)
    s["a0G"][own, 3 * W : 4 * W] = s["attg"][...]
    ag_e("a0")
    rs_b("c4")
    rs_c("c3")

    def gelu_value(v):
        return 0.5 * v * (1.0 + lax.erf(v * 0.7071067811865476))

    def gelu_slope(v):
        return (
            0.5 * (1.0 + lax.erf(v * 0.7071067811865476)) + v * jnp.exp(-0.5 * v * v) * 0.3989422804014327
        )

    part = rs_d("c2")
    s["rawup"][:, 0:UP1] = part
    s["a1G"][own, :] = gelu_value(part).astype(BF)
    ag_e("a1")
    ag_f("a0")
    rs_c("c4")
    part = rs_d("c3")
    s["rawup"][:, UP1:FF] = part
    s["a2G"][own, :] = gelu_value(part).astype(BF)
    ag_e("a2")
    s["a3G"][own, :] = (s["actg"][:, 0:ACT1] * gelu_slope(s["rawup"][:, 0:ACT1])).astype(BF)
    ag_e("a3")
    ag_f("a1")
    part = rs_d("c4").astype(BF).astype(F32)
    s["a4G"][own, :] = (part * gelu_slope(s["rawup"][:, ACT1:FF])).astype(BF)
    ag_e("a4")
    ag_h("a0")
    ag_f("a2")
    ag_h("a1")
    ag_f("a3")
    ag_i("a0")

    score_scale = HEAD_DIM ** (-0.5)

    def head_norm(v):
        cent = v - jnp.mean(v, -1, keepdims=True)
        scale = lax.rsqrt(jnp.mean(cent * cent, -1, keepdims=True) + EPS)
        return cent * scale, scale

    def norm_back(gr, normed_v, scale):
        return scale * (
            gr - jnp.mean(gr, -1, keepdims=True) - normed_v * jnp.mean(gr * normed_v, -1, keepdims=True)
        )

    def head(i):
        lo = i * HEAD_DIM
        hi = lo + HEAD_DIM
        gr = s["a0G"]
        qn, qs = head_norm(gr[:, lo:hi].astype(F32))
        kn, ks = head_norm(gr[:, W + lo : W + hi].astype(F32))
        v = gr[:, 2 * W + lo : 2 * W + hi]
        da = gr[:, 3 * W + lo : 3 * W + hi]
        q, k = qn.astype(BF), kn.astype(BF)
        e = jnp.exp(nt(q, k) * score_scale)
        p = e / jnp.sum(e, -1, keepdims=True)
        pl_ = p.astype(BF)
        s["att"][:, lo:hi] = nn(pl_, v).astype(BF)
        dp = nt(da, v)
        ds = (p * (dp - jnp.sum(dp * p, -1, keepdims=True)) * score_scale).astype(BF)
        s["low"][0, :, lo:hi] = norm_back(nn(ds, k), qn, qs).astype(BF)
        s["low"][1, :, lo:hi] = norm_back(tn(ds, q), kn, ks).astype(BF)
        s["low"][2, :, lo:hi] = tn(pl_, da).astype(BF)

    head(0)
    ag_h("a2")
    ag_f("a4")
    head(1)
    ag_h("a3")
    head(2)
    ag_i("a1")
    ag_i("a2")
    branch = nn(s["att"][...], s["ow"][...])
    branch += nn(s["a1G"][...], s["dw"][0:UP1, :])
    branch += nn(s["a2G"][...], s["dw"][UP1:FF, :])
    s["bQ"][...] = branch.astype(BF)
    ar_1("b")
    ag_h("a4")
    ngrad = nt(s["low"][0], s["aw"][0]) + nt(s["low"][1], s["aw"][1]) + nt(s["low"][2], s["aw"][2])
    s["ng"][...] = ngrad
    ar_2("b")
    s["nrt"][...] = s["nr"][...].T
    for i in range(3):
        s["ag_v"][i] = nn(s["nrt"][...], s["low"][i]).astype(BF)
    ar_3("b")
    ag_i("a3")
    ngrad = s["ng"][...] + nt(s["a3G"][...], s["uw"][:, 0:ACT1])
    ag_i("a4")
    ngrad = ngrad + nt(s["a4G"][...], s["uw"][:, ACT1:FF])
    s["nQ"][...] = ngrad.astype(BF)
    ar_1("n")
    scaled = ngrad * s["gain"][...][None, :]
    sums = pair_sums(scaled, scaled * s["cen"][...])
    sm_cps = ex_start(s["fsy"], sums, y, y_devs)
    ar_2("n")
    s["og_v"][...] = tn(s["att"][...], ups).astype(BF)
    for i in range(0, ACT1, 512):
        s["ug_v"][:, i : i + 512] = nn(s["nrt"][...], s["a3G"][:, i : i + 512]).astype(BF)
    ar_4("b")
    sums = ex_sum(s["fsy"], sm_cps)
    sm_cps = ex_start(s["fsz"], sums, z, z_devs)
    ar_3("n")
    s["ug_v"][:, ACT1:FF] = nn(s["nrt"][...], s["a4G"][...]).astype(BF)
    sums = ex_sum(s["fsz"], sm_cps)
    sm_cps = ex_start(s["fsc"], sums, c, [c_dev])
    for i in range(0, UP1, 384):
        s["dg_v"][i : i + 384, :] = tn(s["a1G"][:, i : i + 384], ups).astype(BF)
    sums = ex_sum(s["fsc"], sm_cps)
    sm_cps = ex_start(s["fsx"], sums, x, x_devs)
    ar_4("n")
    ar_5("b")
    for i in range(0, UP2, 384):
        s["dg_v"][UP1 + i : UP1 + i + 384, :] = tn(s["a2G"][:, i : i + 384], ups).astype(BF)
    sums = ex_sum(s["fsx"], sm_cps)
    sm_cps = ex_start(s["fsh"], sums, h, [h_dev])
    ar_5("n")
    s["lo_v"][...] = (s["tok"][...].astype(F32) + ar_6("b")).astype(BF)
    sums = ex_sum(s["fsh"], sm_cps)
    columns = jnp.concatenate([sums] * 16, 0).T
    grad_mean = columns[:, 0:1] / D
    grad_cross = columns[:, 1:2] / D
    ngrad = ar_6("n")
    centred = s["cen"][...]
    s["gg_v"][...] = jnp.sum(ngrad * centred, 0)
    inner = ngrad * s["gain"][...][None, :] - grad_mean - centred * grad_cross
    s["tg_v"][...] = (ups.astype(F32) + s["inv"][:, 0:1] * inner).astype(BF)

    for cp in copies:
        cp.wait_send()


def hand_on(*refs):
    sem = refs[-1]
    cps = [pltpu.make_async_copy(refs[i], refs[7 + i], sem.at[i]) for i in range(7)]
    for cp in cps:
        cp.start()
    for cp in cps:
        cp.wait()


def body(tokens, norm_gain, attend_weight, up_weight, out_weight, down_weight, upstream):
    any_spec = pl.BlockSpec(memory_space=pl.ANY)
    outs = pl.pallas_call(
        kernel,
        out_shape=(
            pltpu.VMEM((T, W), BF),
            pltpu.VMEM((T, W), BF),
            pltpu.VMEM((W,), F32),
            pltpu.VMEM((3, W, W), BF),
            pltpu.VMEM((W, FF), BF),
            pltpu.VMEM((W, W), BF),
            pltpu.VMEM((FF, W), BF),
        ),
        in_specs=[any_spec] * 7,
        out_specs=(pl.BlockSpec(memory_space=pltpu.VMEM),) * 7,
        scratch_shapes=[pltpu.VMEM(shape, dtype) for shape, dtype in SHAPES.values()]
        + [
            pltpu.SemaphoreType.DMA((N_COPIES,)),
            pltpu.SemaphoreType.DMA((N_COPIES,)),
            pltpu.SemaphoreType.DMA((8,)),
        ],
        compiler_params=pltpu.CompilerParams(
            collective_id=0, has_side_effects=True, vmem_limit_bytes=57 * 1024 * 1024
        ),
        name="layer",
    )(tokens, norm_gain, attend_weight, up_weight, out_weight, down_weight, upstream)
    return pl.pallas_call(
        hand_on,
        out_shape=tuple(jax.ShapeDtypeStruct(o.shape, o.dtype) for o in outs),
        in_specs=[any_spec] * 7,
        out_specs=(any_spec,) * 7,
        scratch_shapes=[pltpu.SemaphoreType.DMA((7,))],
        compiler_params=pltpu.CompilerParams(vmem_limit_bytes=2 * 1024 * 1024),
        name="hand_on",
    )(*outs)


def solution(mesh):
    return jax.shard_map(
        body,
        mesh=mesh,
        in_specs=(
            P(None, "fin"),
            P("fin"),
            P(None, "fin", "fout"),
            P("fin", "fout"),
            P("fout", "fin"),
            P("fout", "fin"),
            P(None, "fin"),
        ),
        out_specs=(
            P(None, "fin"),
            P(None, "fin"),
            P("fin"),
            P(None, "fin", "fout"),
            P("fin", "fout"),
            P("fout", "fin"),
            P("fout", "fin"),
        ),
        check_vma=False,
    )
```

```python
import jax
import jax.numpy as jnp
from jax import lax
from jax.experimental import pallas as pl
from jax.experimental.pallas import tpu as pltpu
from jax.sharding import PartitionSpec as P

D = 6144
HEAD_DIM = 128
T = 256
W = 384
FF = 1536
EPS = 1e-06
BF = jnp.bfloat16
F32 = jnp.float32
MESH = pl.DeviceIdType.MESH
HIGH = lax.Precision.HIGHEST

WIDE = 1024
NARROW = FF - WIDE
UP = ((0, WIDE), (WIDE, NARROW))
HEADS = (0, 1, 2)
CHUNKS = {"h1": 512, "h2": 512, "u0": WIDE, "u1": NARROW, "d0": WIDE, "d1": NARROW}
GROUPS = {"h0": 512, "h1": 512, "h2": 512, "a0": WIDE, "a1": NARROW, "l0": WIDE}


def scratch_shapes():
    shapes = {
        "tok": ((T, W), BF),
        "gain": ((W,), F32),
        "aw": ((3, W, W), BF),
        "uw": ((W, FF), BF),
        "ow": ((W, W), BF),
        "dw": ((FF, W), BF),
        "ups": ((T, W), BF),
        "st": ((16, 8, 128), F32),
        "wg": ((4, 24, 128), F32),
        "wz": ((4, 8, 128), F32),
        "h0P": ((4, 4, 16, 512), BF),
        "h0Z": ((3, 4, 16, 512), BF),
        "h0S": ((4, 16, 512), BF),
        "h0Y": ((3, 16, 512), BF),
        "l1G": ((4, 4, 16, NARROW), BF),
        "col": ((T, 128), F32),
        "nrt": ((W, T), BF),
        "cen": ((T, W), F32),
        "rawup": ((16, FF), F32),
        "att": ((T, W), BF),
        "low": ((3, T, W), BF),
        "ng": ((T, W), F32),
        "fa": ((16, 8, 128), F32),
        "fb": ((2, 8, 128), F32),
        "fc": ((8, 8, 128), F32),
    }
    for name, w in CHUNKS.items():
        shapes[name + "P"] = ((T, w), BF)
        shapes[name + "R1"] = ((2, 32, w), BF)
        shapes[name + "R2"] = ((2, 64, w), BF)
        shapes[name + "T"] = ((2, 32, w), BF)
        shapes[name + "S"] = ((64, w), BF)
        shapes[name + "Z"] = ((3, 16, w), BF)
    for name, w in GROUPS.items():
        shapes[name + "G"] = ((T, w), BF)
    for name in ("b", "n"):
        shapes[name + "Q"] = ((T, W), BF)
        shapes[name + "AC"] = ((128, W), BF)
        shapes[name + "H1"] = ((128, W), BF)
        shapes[name + "AX"] = ((7, 16, W), BF)
        shapes[name + "R"] = ((T, W), BF)
    return shapes


SHAPES = scratch_shapes()
N_COPIES = 200


def nt(a, b, **kw):
    return lax.dot_general(a, b, (((1,), (1,)), ((), ())), preferred_element_type=F32, **kw)


def tn(a, b):
    return lax.dot_general(a, b, (((0,), (0,)), ((), ())), preferred_element_type=F32)


def nn(a, b):
    return jnp.dot(a, b, preferred_element_type=F32)


def rows(start, size):
    return pl.ds(pl.multiple_of(start, 16), size)


def kernel(tok_h, gain_h, aw_h, uw_h, ow_h, dw_h, ups_h, *refs):
    outs, scr = refs[:7], refs[7:]
    s = dict(zip(SHAPES, scr[: len(SHAPES)]))
    s.update(zip(("lo_v", "tg_v", "gg_v", "ag_v", "ug_v", "og_v", "dg_v"), outs))
    send_sem, recv_sem, load_sem = scr[len(SHAPES) :]

    f = lax.axis_index("fin")
    g = lax.axis_index("fout")
    y, z = f // 4, f % 4
    x, h, c = g // 4, (g // 2) % 2, g % 2

    def fin_dev(yy, zz):
        return (yy * 4 + zz, g)

    def fout_dev(xx, hh, cc):
        return (f, xx * 4 + hh * 2 + cc)

    right, left = lax.rem(y + 1, 4), lax.rem(y + 3, 4)
    far = lax.rem(y + 2, 4)
    dev_right, dev_left = fin_dev(right, z), fin_dev(left, z)
    y_devs = [fin_dev(lax.rem(y + d, 4), z) for d in (1, 2, 3)]
    z_devs = [fin_dev(y, lax.rem(z + d, 4)) for d in (1, 2, 3)]
    xh = x * 2 + h
    xh_devs = []
    for d in range(1, 8):
        other = lax.rem(xh + d, 8)
        xh_devs.append(fout_dev(other // 2, lax.rem(other, 2), c))
    c_dev = fout_dev(x, h, 1 - c)
    fin_devs = [(lax.rem(f + d, 16), g) for d in range(1, 16)]
    peers = fin_devs + xh_devs + [c_dev]

    loads = {}
    for i, (name, src) in enumerate(
        [("tok", tok_h), ("gain", gain_h), ("aw", aw_h), ("ups", ups_h), ("ow", ow_h), ("uw", uw_h), ("dw", dw_h)]
    ):
        loads[name] = pltpu.make_async_copy(src, s[name], load_sem.at[i])
        loads[name].start()

    barrier = pltpu.get_barrier_semaphore()
    for dev in peers:
        pl.semaphore_signal(barrier, inc=1, device_id=dev, device_id_type=MESH)

    copies = []

    def rcopy(src, dst, dev):
        i = len(copies)
        cp = pltpu.make_async_remote_copy(
            src_ref=src,
            dst_ref=dst,
            send_sem=send_sem.at[i],
            recv_sem=recv_sem.at[i],
            device_id=dev,
            device_id_type=MESH,
        )
        cp.start()
        copies.append(cp)
        return cp

    pending = {}

    def rs_a(n):
        p, r1, r2 = s[n + "P"], s[n + "R1"], s[n + "R2"]
        pending[n + "r1"] = [
            rcopy(p.at[rows(far * 64, 32)], r1.at[0], dev_right),
            rcopy(p.at[rows(far * 64 + 32, 32)], r1.at[1], dev_left),
        ]
        pending[n + "r2"] = [
            rcopy(p.at[rows(right * 64 + 32, 32)], r2.at[0, pl.ds(32, 32)], dev_right),
            rcopy(p.at[rows(left * 64, 32)], r2.at[1, pl.ds(0, 32)], dev_left),
        ]

    def rs_b(n):
        p, r1, r2, t = s[n + "P"], s[n + "R1"], s[n + "R2"], s[n + "T"]
        first, second = pending[n + "r1"]
        first.wait_recv()
        t[0] = (p[rows(right * 64, 32)].astype(F32) + r1[0].astype(F32)).astype(BF)
        pending[n + "r2"].append(rcopy(t.at[0], r2.at[0, pl.ds(0, 32)], dev_right))
        second.wait_recv()
        t[1] = (p[rows(left * 64 + 32, 32)].astype(F32) + r1[1].astype(F32)).astype(BF)
        pending[n + "r2"].append(rcopy(t.at[1], r2.at[1, pl.ds(32, 32)], dev_left))

    def rs_c(n, blocks=()):
        p, r2, sm, zz = s[n + "P"], s[n + "R2"], s[n + "S"], s[n + "Z"]
        for cp in pending[n + "r2"]:
            cp.wait_recv()
        total = p[rows(y * 64, 64)].astype(F32) + r2[0].astype(F32) + r2[1].astype(F32)
        if blocks:
            shift = s["col"][rows(y * 64, 64), :]
            shift = [jnp.broadcast_to(shift[:, 2 + i : 3 + i], (64, 128)) for i in range(4)]
            parts = [
                sum(shift[i] * s["wg"][i, b : b + 1, :] for i in range(4)) for b in blocks
            ]
            wide = len(blocks) * 128
            sm[:, 0:wide] = (total[:, 0:wide] + jnp.concatenate(parts, 1)).astype(BF)
            if wide < total.shape[1]:
                sm[:, wide:] = total[:, wide:].astype(BF)
        else:
            sm[...] = total.astype(BF)
        pending[n + "z"] = [
            rcopy(sm.at[rows(lax.rem(z + d, 4) * 16, 16)], zz.at[d - 1], z_devs[d - 1]) for d in (1, 2, 3)
        ]

    def rs_d(n):
        sm, zz = s[n + "S"], s[n + "Z"]
        for cp in pending[n + "z"]:
            cp.wait_recv()
        return (
            sm[rows(z * 16, 16)].astype(F32) + zz[0].astype(F32) + zz[1].astype(F32) + zz[2].astype(F32)
        )

    def rs_za(n):
        p = s[n + "P"]
        pending[n + "z"] = [
            rcopy(p.at[:, lax.rem(z + d, 4)], s[n + "Z"].at[d - 1], z_devs[d - 1]) for d in (1, 2, 3)
        ]

    def rs_zc(n, blocks):
        p, zz, sm = s[n + "P"], s[n + "Z"], s[n + "S"]
        for cp in pending[n + "z"]:
            cp.wait_recv()
        for q in range(4):
            total = p[q, z].astype(F32) + zz[0, q].astype(F32) + zz[1, q].astype(F32) + zz[2, q].astype(F32)
            shift = s["col"][rows(q * 64 + z * 16, 16), :]
            shift = [jnp.broadcast_to(shift[:, 6 + i : 7 + i], (16, 128)) for i in range(4)]
            parts = [sum(shift[i] * s["wz"][i, b : b + 1, :] for i in range(4)) for b in blocks]
            wide = len(blocks) * 128
            sm[q, :, 0:wide] = (total[:, 0:wide] + jnp.concatenate(parts, 1)).astype(BF)
            sm[q, :, wide:] = total[:, wide:].astype(BF)
        pending[n + "y"] = [
            rcopy(sm.at[lax.rem(y + d, 4)], s[n + "Y"].at[d - 1], y_devs[d - 1]) for d in (1, 2, 3)
        ]

    def rs_zd(n):
        yy = s[n + "Y"]
        for cp in pending[n + "y"]:
            cp.wait_recv()
        return s[n + "S"][y].astype(F32) + yy[0].astype(F32) + yy[1].astype(F32) + yy[2].astype(F32)

    def ag_ye(n):
        own_block = s[n + "G"].at[y, z]
        pending[n + "e"] = [rcopy(own_block, own_block, dev) for dev in y_devs]

    def ag_yf(n):
        for cp in pending[n + "e"]:
            cp.wait_recv()
        block = s[n + "G"].at[:, z]
        pending[n + "h"] = [rcopy(block, block, dev) for dev in z_devs]

    def ag_e(n):
        gr = s[n + "G"]
        own = gr.at[rows(f * 16, 16)]
        pending[n + "e"] = [rcopy(own, own, dev) for dev in z_devs]

    def ag_f(n):
        gr = s[n + "G"]
        for cp in pending[n + "e"]:
            cp.wait_recv()
        block = gr.at[rows(y * 64, 64)]
        pending[n + "f"] = [rcopy(block, block, dev_right), rcopy(block, block, dev_left)]

    def ag_h(n):
        gr = s[n + "G"]
        first, second = pending[n + "f"]
        first.wait_recv()
        one = gr.at[rows(left * 64, 32)]
        cps = [rcopy(one, one, dev_right)]
        second.wait_recv()
        two = gr.at[rows(right * 64 + 32, 32)]
        cps.append(rcopy(two, two, dev_left))
        pending[n + "h"] = cps

    def ag_i(n):
        for cp in pending[n + "h"]:
            cp.wait_recv()

    def ar_1(n):
        q = s[n + "Q"]
        pending[n + "1"] = rcopy(q.at[rows((1 - c) * 128, 128)], s[n + "AC"], c_dev)

    def ar_2(n):
        q, h1, ax = s[n + "Q"], s[n + "H1"], s[n + "AX"]
        pending[n + "1"].wait_recv()
        h1[...] = (q[rows(c * 128, 128)].astype(F32) + s[n + "AC"][...].astype(F32)).astype(BF)
        pending[n + "2"] = [
            rcopy(h1.at[rows(lax.rem(xh + d, 8) * 16, 16)], ax.at[d - 1], xh_devs[d - 1]) for d in range(1, 8)
        ]

    def ar_3(n):
        h1, ax, res = s[n + "H1"], s[n + "AX"], s[n + "R"]
        for cp in pending[n + "2"]:
            cp.wait_recv()
        total = h1[rows(xh * 16, 16)].astype(F32) + sum(ax[i].astype(F32) for i in range(7))
        at = rows(c * 128 + xh * 16, 16)
        res[at] = total.astype(BF)
        pending[n + "3"] = [rcopy(res.at[at], res.at[at], dev) for dev in xh_devs]

    def ar_4(n):
        res = s[n + "R"]
        for cp in pending[n + "3"]:
            cp.wait_recv()
        at = res.at[rows(c * 128, 128)]
        pending[n + "4"] = rcopy(at, at, c_dev)

    def ar_5(n):
        pending[n + "4"].wait_recv()
        return s[n + "R"][...].astype(F32)

    def ex_start(buf, value, slot, devs):
        one = buf.at[slot]
        one[0:2, :] = value[0:2, 0:128]
        one[2:4, :] = value[0:2, 128:256]
        return [rcopy(one, one, dev) for dev in devs]

    def ex_sum(buf, cps):
        for cp in cps:
            cp.wait_recv()
        total = sum(buf[i] for i in range(buf.shape[0]))
        return jnp.concatenate([total[0:2, :], total[2:4, :]], 1)

    row_id = lax.broadcasted_iota(jnp.int32, (8, W), 0)
    pick0 = jnp.where(row_id == 0, 1.0, 0.0).astype(F32)
    pick1 = jnp.where(row_id == 1, 1.0, 0.0).astype(F32)

    def pair_sums(first, second):
        return nt(pick0, first, precision=HIGH) + nt(pick1, second, precision=HIGH)

    loads["tok"].wait()
    inputs = s["tok"][...].astype(F32)
    stats = pair_sums(inputs, inputs * inputs)
    stat = s["st"].at[f]
    stat[0:2, :] = stats[0:2, 0:128]
    stat[2:4, :] = stats[0:2, 128:256]
    local = (inputs - jnp.mean(inputs, 1, keepdims=True))
    loads["gain"].wait()
    gain = s["gain"][...][None, :]
    local = (local * gain).astype(BF)
    gain_high = gain.astype(BF).astype(F32)
    row16 = lax.broadcasted_iota(jnp.int32, (16, W), 0)
    gain_rows = jnp.where(row16 == 0, gain_high, jnp.where(row16 == 1, gain - gain_high, 0.0)).astype(BF)
    wg = s["wg"].at[y]
    wz = s["wz"].at[z]

    def gain_product(weight):
        both = nn(gain_rows, weight)
        return both[0:1, :] + both[1:2, :]

    loads["aw"].wait()
    for i in range(3):
        line = gain_product(s["aw"][i])
        part = nn(local, s["aw"][i]).astype(BF)
        for k in HEADS:
            wg[3 * k + i : 3 * k + i + 1, :] = line[:, k * 128 : (k + 1) * 128]
        wz[i : i + 1, :] = line[:, 0:128]
        s["h0P"][:, :, :, i * 128 : (i + 1) * 128] = part[:, 0:128].reshape(4, 4, 16, 128)
        for k in (1, 2):
            s[f"h{k}P"][:, i * 128 : (i + 1) * 128] = part[:, k * 128 : (k + 1) * 128]
    loads["ups"].wait()
    loads["ow"].wait()
    ups = s["ups"][...]
    part = nt(ups, s["ow"][...]).astype(BF)
    s["h0P"][:, :, :, W:512] = part[:, 0:128].reshape(4, 4, 16, 128)
    for k in (1, 2):
        s[f"h{k}P"][:, W:512] = part[:, k * 128 : (k + 1) * 128]
    loads["uw"].wait()
    for i in range(4):
        line = gain_product(s["uw"][:, i * W : (i + 1) * W])
        for k in range(3):
            wg[9 + 3 * i + k : 10 + 3 * i + k, :] = line[:, k * 128 : (k + 1) * 128]

    def up_product(k):
        for i in range(0, UP[k][1], 512):
            at = UP[k][0] + i
            s[f"u{k}P"][:, i : i + 512] = nn(local, s["uw"][:, at : at + 512]).astype(BF)

    def down_product(k):
        for i in range(0, UP[k][1], 512):
            at = UP[k][0] + i
            s[f"d{k}P"][:, i : i + 512] = nt(ups, s["dw"][at : at + 512, :]).astype(BF)

    up_product(0)
    pl.semaphore_wait(barrier, len(peers))
    rs_za("h0")
    st_cps = [rcopy(stat, stat, dev) for dev in fin_devs]
    wg_cps = [rcopy(wg, wg, dev) for dev in y_devs]
    rs_a("h1")
    rs_a("h2")
    wg_cps += [rcopy(wz, wz, dev) for dev in z_devs]
    rs_a("u0")
    up_product(1)
    rs_b("h1")
    rs_a("u1")
    for cp in st_cps:
        cp.wait_recv()
    total = sum(s["st"][i] for i in range(16))
    mean_row = jnp.concatenate([total[0:1, :], total[2:3, :]], 1) / D
    square_row = jnp.concatenate([total[1:2, :], total[3:4, :]], 1) / D
    inv_row = lax.rsqrt(square_row - mean_row * mean_row + EPS)
    lines = [mean_row, inv_row]
    for i in range(8):
        one = s["st"][i * 4 + z] if i < 4 else s["st"][y * 4 + i - 4]
        lines.append(jnp.concatenate([one[0:1, :], one[2:3, :]], 1) / W - mean_row)
    lines += [mean_row] * 6
    s["col"][...] = jnp.concatenate(lines * 8, 0).T
    rs_b("h2")
    loads["dw"].wait()
    down_product(0)
    rs_a("d0")
    for cp in wg_cps:
        cp.wait_recv()
    rs_zc("h0", (0, 1, 2))
    rs_b("u0")
    rs_c("h1", (3, 4, 5))
    down_product(1)
    rs_a("d1")
    rs_b("u1")
    rs_c("h2", (6, 7, 8))
    own = rows(f * 16, 16)
    own_inv = s["col"][own, 1:2]

    def head_rows(k):
        part = rs_d(f"h{k}") if k else rs_zd("h0")
        s[f"h{k}G"][own, 0:W] = (part[:, 0:W] * own_inv).astype(BF)
        s[f"h{k}G"][own, W:512] = part[:, W:512].astype(BF)
        ag_e(f"h{k}")

    def up_rows(k):
        part = rs_d(f"u{k}") * own_inv
        s["rawup"][:, UP[k][0] : UP[k][0] + UP[k][1]] = part
        s[f"a{k}G"][own, :] = gelu_value(part).astype(BF)
        ag_e(f"a{k}")

    def low_rows(k):
        part = rs_d(f"d{k}").astype(BF).astype(F32)
        part = (part * gelu_slope(s["rawup"][:, UP[k][0] : UP[k][0] + UP[k][1]])).astype(BF)
        if k == 0:
            s["l0G"][own, :] = part
            ag_e("l0")
        else:
            s["l1G"][y, z] = part
            ag_ye("l1")

    def gelu_value(v):
        return 0.5 * v * (1.0 + lax.erf(v * 0.7071067811865476))

    def gelu_slope(v):
        return (
            0.5 * (1.0 + lax.erf(v * 0.7071067811865476)) + v * jnp.exp(-0.5 * v * v) * 0.3989422804014327
        )

    head_rows(0)
    rs_b("d0")
    head_rows(1)
    rs_c("u0", tuple(range(9, 17)))
    rs_b("d1")
    head_rows(2)
    rs_c("u1", tuple(range(17, 21)))
    ag_f("h0")
    rs_c("d0")
    ag_f("h1")
    rs_c("d1")
    up_rows(0)
    ag_f("h2")
    up_rows(1)
    ag_h("h0")
    low_rows(0)
    ag_h("h1")
    low_rows(1)
    ag_f("a0")
    ag_h("h2")
    ag_f("a1")
    ag_i("h0")
    centred = (inputs - s["col"][:, 0:1]) * s["col"][:, 1:2]
    s["cen"][...] = centred
    normed = (centred * gain).astype(BF)
    s["nrt"][...] = normed.T
    ag_f("l0")
    ag_yf("l1")
    ag_h("a0")

    score_scale = HEAD_DIM ** (-0.5)

    def head_norm(v):
        cent = v - jnp.mean(v, -1, keepdims=True)
        scale = lax.rsqrt(jnp.mean(cent * cent, -1, keepdims=True) + EPS)
        return cent * scale, scale

    def norm_back(gr, normed_v, scale):
        return scale * (
            gr - jnp.mean(gr, -1, keepdims=True) - normed_v * jnp.mean(gr * normed_v, -1, keepdims=True)
        )

    def head(i):
        lo = i * HEAD_DIM
        hi = lo + HEAD_DIM
        gr = s[f"h{i}G"]
        qn, qs = head_norm(gr[:, 0:128].astype(F32))
        kn, ks = head_norm(gr[:, 128:256].astype(F32))
        v = gr[:, 256:384]
        da = gr[:, 384:512]
        q, k = qn.astype(BF), kn.astype(BF)
        e = jnp.exp(nt(q, k) * score_scale)
        p = e / jnp.sum(e, -1, keepdims=True)
        pl_ = p.astype(BF)
        s["att"][:, lo:hi] = nn(pl_, v).astype(BF)
        dp = nt(da, v)
        ds = (p * (dp - jnp.sum(dp * p, -1, keepdims=True)) * score_scale).astype(BF)
        s["low"][0, :, lo:hi] = norm_back(nn(ds, k), qn, qs).astype(BF)
        s["low"][1, :, lo:hi] = norm_back(tn(ds, q), kn, ks).astype(BF)
        s["low"][2, :, lo:hi] = tn(pl_, da).astype(BF)

    head(0)
    ag_h("a1")
    ag_i("h1")
    head(1)
    ag_h("l0")
    ag_i("h2")
    head(2)
    ag_i("a0")
    branch = nn(s["att"][...], s["ow"][...]) + nn(s["a0G"][...], s["dw"][0:WIDE, :])
    ag_i("a1")
    s["bQ"][...] = (branch + nn(s["a1G"][...], s["dw"][WIDE:FF, :])).astype(BF)
    ar_1("b")
    ngrad = nt(s["low"][0], s["aw"][0]) + nt(s["low"][1], s["aw"][1]) + nt(s["low"][2], s["aw"][2])
    ag_i("l0")
    s["ng"][...] = ngrad + nt(s["l0G"][...], s["uw"][:, 0:WIDE])
    ar_2("b")
    ag_i("l1")
    l1_rows = s["l1G"][...].reshape(T, NARROW)
    ngrad = s["ng"][...] + nt(l1_rows, s["uw"][:, WIDE:FF])
    s["nQ"][...] = ngrad.astype(BF)
    ar_1("n")
    scaled = ngrad * gain
    sums = pair_sums(scaled, scaled * s["cen"][...])
    sm_cps = ex_start(s["fa"], sums, f, fin_devs)
    ar_2("n")
    for i in range(3):
        s["ag_v"][i] = nn(s["nrt"][...], s["low"][i]).astype(BF)
    s["og_v"][...] = tn(s["att"][...], ups).astype(BF)
    ar_3("b")
    sums = ex_sum(s["fa"], sm_cps)
    sm_cps = ex_start(s["fb"], sums, c, [c_dev])
    ar_3("n")
    sums = ex_sum(s["fb"], sm_cps)
    sm_cps = ex_start(s["fc"], sums, xh, xh_devs)
    for i in (0, 512):
        s["ug_v"][:, i : i + 512] = nn(s["nrt"][...], s["l0G"][:, i : i + 512]).astype(BF)
    s["ug_v"][:, WIDE:FF] = nn(s["nrt"][...], l1_rows).astype(BF)
    ar_4("b")
    for i in (0, 512):
        s["dg_v"][i : i + 512, :] = tn(s["a0G"][:, i : i + 512], ups).astype(BF)
    s["dg_v"][WIDE:FF, :] = tn(s["a1G"][...], ups).astype(BF)
    s["lo_v"][...] = (s["tok"][...].astype(F32) + ar_5("b")).astype(BF)
    ar_4("n")
    sums = ex_sum(s["fc"], sm_cps)
    columns = jnp.concatenate([sums] * 64, 0).T
    grad_mean = columns[:, 0:1] / D
    grad_cross = columns[:, 1:2] / D
    ngrad = ar_5("n")
    centred = s["cen"][...]
    s["gg_v"][...] = jnp.sum(ngrad * centred, 0)
    inner = ngrad * gain - grad_mean - centred * grad_cross
    s["tg_v"][...] = (ups.astype(F32) + s["col"][:, 1:2] * inner).astype(BF)

    for cp in copies:
        cp.wait_send()


def hand_on(*refs):
    sem = refs[-1]
    cps = [pltpu.make_async_copy(refs[i], refs[7 + i], sem.at[i]) for i in range(7)]
    for cp in cps:
        cp.start()
    for cp in cps:
        cp.wait()


def body(tokens, norm_gain, attend_weight, up_weight, out_weight, down_weight, upstream):
    any_spec = pl.BlockSpec(memory_space=pl.ANY)
    outs = pl.pallas_call(
        kernel,
        out_shape=(
            pltpu.VMEM((T, W), BF),
            pltpu.VMEM((T, W), BF),
            pltpu.VMEM((W,), F32),
            pltpu.VMEM((3, W, W), BF),
            pltpu.VMEM((W, FF), BF),
            pltpu.VMEM((W, W), BF),
            pltpu.VMEM((FF, W), BF),
        ),
        in_specs=[any_spec] * 7,
        out_specs=(pl.BlockSpec(memory_space=pltpu.VMEM),) * 7,
        scratch_shapes=[pltpu.VMEM(shape, dtype) for shape, dtype in SHAPES.values()]
        + [
            pltpu.SemaphoreType.DMA((N_COPIES,)),
            pltpu.SemaphoreType.DMA((N_COPIES,)),
            pltpu.SemaphoreType.DMA((8,)),
        ],
        compiler_params=pltpu.CompilerParams(
            collective_id=0, has_side_effects=True, vmem_limit_bytes=57 * 1024 * 1024
        ),
        name="layer",
    )(tokens, norm_gain, attend_weight, up_weight, out_weight, down_weight, upstream)
    return pl.pallas_call(
        hand_on,
        out_shape=tuple(jax.ShapeDtypeStruct(o.shape, o.dtype) for o in outs),
        in_specs=[any_spec] * 7,
        out_specs=(any_spec,) * 7,
        scratch_shapes=[pltpu.SemaphoreType.DMA((7,))],
        compiler_params=pltpu.CompilerParams(vmem_limit_bytes=2 * 1024 * 1024),
        name="hand_on",
    )(*outs)


def solution(mesh):
    return jax.shard_map(
        body,
        mesh=mesh,
        in_specs=(
            P(None, "fin"),
            P("fin"),
            P(None, "fin", "fout"),
            P("fin", "fout"),
            P("fout", "fin"),
            P("fout", "fin"),
            P(None, "fin"),
        ),
        out_specs=(
            P(None, "fin"),
            P(None, "fin"),
            P("fin"),
            P(None, "fin", "fout"),
            P("fin", "fout"),
            P("fout", "fin"),
            P("fout", "fin"),
        ),
        check_vma=False,
    )
```

```python
import jax
import jax.numpy as jnp
from jax import lax
from jax.experimental import pallas as pl
from jax.experimental.pallas import tpu as pltpu
from jax.sharding import PartitionSpec as P

D = 6144
HEAD_DIM = 128
T = 256
W = 384
FF = 1536
EPS = 1e-06
BF = jnp.bfloat16
F32 = jnp.float32
MESH = pl.DeviceIdType.MESH
HIGH = lax.Precision.HIGHEST

WIDE = 768
NARROW = FF - WIDE
UP = ((0, WIDE), (WIDE, NARROW))
HEADS = (0, 1, 2)
CHUNKS = {"h1": 512, "h2": 512, "u0": WIDE, "u1": NARROW, "d0": WIDE, "d1": NARROW}
GROUPS = {"h0": 512, "h1": 512, "h2": 512, "a0": WIDE, "a1": NARROW, "l0": WIDE}


def scratch_shapes():
    shapes = {
        "tok": ((T, W), BF),
        "gain": ((W,), F32),
        "aw": ((3, W, W), BF),
        "uw": ((W, FF), BF),
        "ow": ((W, W), BF),
        "dw": ((FF, W), BF),
        "ups": ((T, W), BF),
        "st": ((16, 8, 128), F32),
        "wg": ((4, 24, 128), F32),
        "wz": ((4, 8, 128), F32),
        "h0P": ((4, 4, 16, 512), BF),
        "h0Z": ((3, 4, 16, 512), BF),
        "h0S": ((4, 16, 512), BF),
        "h0Y": ((3, 16, 512), BF),
        "l1G": ((4, 4, 16, NARROW), BF),
        "col": ((T, 128), F32),
        "nrt": ((W, T), BF),
        "cen": ((T, W), F32),
        "rawup": ((16, FF), F32),
        "att": ((T, W), BF),
        "low": ((3, T, W), BF),
        "ng": ((T, W), F32),
        "fa": ((16, 8, 128), F32),
        "fb": ((2, 8, 128), F32),
        "fc": ((8, 8, 128), F32),
    }
    for name, w in CHUNKS.items():
        shapes[name + "P"] = ((T, w), BF)
        shapes[name + "R1"] = ((2, 32, w), BF)
        shapes[name + "R2"] = ((2, 64, w), BF)
        shapes[name + "T"] = ((2, 32, w), BF)
        shapes[name + "S"] = ((64, w), BF)
        shapes[name + "Z"] = ((3, 16, w), BF)
    for name, w in GROUPS.items():
        shapes[name + "G"] = ((T, w), BF)
    for name in ("b", "n"):
        shapes[name + "Q"] = ((T, W), BF)
        shapes[name + "AC"] = ((128, W), BF)
        shapes[name + "H1"] = ((128, W), BF)
        shapes[name + "AX"] = ((7, 16, W), BF)
        shapes[name + "R"] = ((T, W), BF)
    return shapes


SHAPES = scratch_shapes()
N_COPIES = 200


def nt(a, b, **kw):
    return lax.dot_general(a, b, (((1,), (1,)), ((), ())), preferred_element_type=F32, **kw)


def tn(a, b):
    return lax.dot_general(a, b, (((0,), (0,)), ((), ())), preferred_element_type=F32)


def nn(a, b):
    return jnp.dot(a, b, preferred_element_type=F32)


def rows(start, size):
    return pl.ds(pl.multiple_of(start, 16), size)


def kernel(tok_h, gain_h, aw_h, uw_h, ow_h, dw_h, ups_h, *refs):
    outs, scr = refs[:7], refs[7:]
    s = dict(zip(SHAPES, scr[: len(SHAPES)]))
    s.update(zip(("lo_v", "tg_v", "gg_v", "ag_v", "ug_v", "og_v", "dg_v"), outs))
    send_sem, recv_sem, load_sem = scr[len(SHAPES) :]

    f = lax.axis_index("fin")
    g = lax.axis_index("fout")
    y, z = f // 4, f % 4
    x, h, c = g // 4, (g // 2) % 2, g % 2

    def fin_dev(yy, zz):
        return (yy * 4 + zz, g)

    def fout_dev(xx, hh, cc):
        return (f, xx * 4 + hh * 2 + cc)

    right, left = lax.rem(y + 1, 4), lax.rem(y + 3, 4)
    far = lax.rem(y + 2, 4)
    dev_right, dev_left = fin_dev(right, z), fin_dev(left, z)
    y_devs = [fin_dev(lax.rem(y + d, 4), z) for d in (1, 2, 3)]
    z_devs = [fin_dev(y, lax.rem(z + d, 4)) for d in (1, 2, 3)]
    xh = x * 2 + h
    xh_devs = []
    for d in range(1, 8):
        other = lax.rem(xh + d, 8)
        xh_devs.append(fout_dev(other // 2, lax.rem(other, 2), c))
    c_dev = fout_dev(x, h, 1 - c)
    fin_devs = [(lax.rem(f + d, 16), g) for d in range(1, 16)]
    peers = fin_devs + xh_devs + [c_dev]

    loads = {}
    for i, (name, src) in enumerate(
        [("tok", tok_h), ("gain", gain_h), ("aw", aw_h), ("ups", ups_h), ("ow", ow_h), ("uw", uw_h), ("dw", dw_h)]
    ):
        loads[name] = pltpu.make_async_copy(src, s[name], load_sem.at[i])
        loads[name].start()

    barrier = pltpu.get_barrier_semaphore()
    for dev in peers:
        pl.semaphore_signal(barrier, inc=1, device_id=dev, device_id_type=MESH)

    copies = []

    def rcopy(src, dst, dev):
        i = len(copies)
        cp = pltpu.make_async_remote_copy(
            src_ref=src,
            dst_ref=dst,
            send_sem=send_sem.at[i],
            recv_sem=recv_sem.at[i],
            device_id=dev,
            device_id_type=MESH,
        )
        cp.start()
        copies.append(cp)
        return cp

    pending = {}

    def rs_a(n):
        p, r1, r2 = s[n + "P"], s[n + "R1"], s[n + "R2"]
        pending[n + "r1"] = [
            rcopy(p.at[rows(far * 64, 32)], r1.at[0], dev_right),
            rcopy(p.at[rows(far * 64 + 32, 32)], r1.at[1], dev_left),
        ]
        pending[n + "r2"] = [
            rcopy(p.at[rows(right * 64 + 32, 32)], r2.at[0, pl.ds(32, 32)], dev_right),
            rcopy(p.at[rows(left * 64, 32)], r2.at[1, pl.ds(0, 32)], dev_left),
        ]

    def rs_b(n):
        p, r1, r2, t = s[n + "P"], s[n + "R1"], s[n + "R2"], s[n + "T"]
        first, second = pending[n + "r1"]
        first.wait_recv()
        t[0] = (p[rows(right * 64, 32)].astype(F32) + r1[0].astype(F32)).astype(BF)
        pending[n + "r2"].append(rcopy(t.at[0], r2.at[0, pl.ds(0, 32)], dev_right))
        second.wait_recv()
        t[1] = (p[rows(left * 64 + 32, 32)].astype(F32) + r1[1].astype(F32)).astype(BF)
        pending[n + "r2"].append(rcopy(t.at[1], r2.at[1, pl.ds(32, 32)], dev_left))

    def rs_c(n, blocks=()):
        p, r2, sm, zz = s[n + "P"], s[n + "R2"], s[n + "S"], s[n + "Z"]
        for cp in pending[n + "r2"]:
            cp.wait_recv()
        total = p[rows(y * 64, 64)].astype(F32) + r2[0].astype(F32) + r2[1].astype(F32)
        if blocks:
            shift = s["col"][rows(y * 64, 64), :]
            shift = [jnp.broadcast_to(shift[:, 2 + i : 3 + i], (64, 128)) for i in range(4)]
            parts = [
                sum(shift[i] * s["wg"][i, b : b + 1, :] for i in range(4)) for b in blocks
            ]
            wide = len(blocks) * 128
            sm[:, 0:wide] = (total[:, 0:wide] + jnp.concatenate(parts, 1)).astype(BF)
            if wide < total.shape[1]:
                sm[:, wide:] = total[:, wide:].astype(BF)
        else:
            sm[...] = total.astype(BF)
        pending[n + "z"] = [
            rcopy(sm.at[rows(lax.rem(z + d, 4) * 16, 16)], zz.at[d - 1], z_devs[d - 1]) for d in (1, 2, 3)
        ]

    def rs_d(n):
        sm, zz = s[n + "S"], s[n + "Z"]
        for cp in pending[n + "z"]:
            cp.wait_recv()
        return (
            sm[rows(z * 16, 16)].astype(F32) + zz[0].astype(F32) + zz[1].astype(F32) + zz[2].astype(F32)
        )

    def rs_za(n):
        p = s[n + "P"]
        pending[n + "z"] = [
            rcopy(p.at[:, lax.rem(z + d, 4)], s[n + "Z"].at[d - 1], z_devs[d - 1]) for d in (1, 2, 3)
        ]

    def rs_zc(n, blocks):
        p, zz, sm = s[n + "P"], s[n + "Z"], s[n + "S"]
        for cp in pending[n + "z"]:
            cp.wait_recv()
        for q in range(4):
            total = p[q, z].astype(F32) + zz[0, q].astype(F32) + zz[1, q].astype(F32) + zz[2, q].astype(F32)
            shift = s["col"][rows(q * 64 + z * 16, 16), :]
            shift = [jnp.broadcast_to(shift[:, 6 + i : 7 + i], (16, 128)) for i in range(4)]
            parts = [sum(shift[i] * s["wz"][i, b : b + 1, :] for i in range(4)) for b in blocks]
            wide = len(blocks) * 128
            sm[q, :, 0:wide] = (total[:, 0:wide] + jnp.concatenate(parts, 1)).astype(BF)
            sm[q, :, wide:] = total[:, wide:].astype(BF)
        pending[n + "y"] = [
            rcopy(sm.at[lax.rem(y + d, 4)], s[n + "Y"].at[d - 1], y_devs[d - 1]) for d in (1, 2, 3)
        ]

    def rs_zd(n):
        yy = s[n + "Y"]
        for cp in pending[n + "y"]:
            cp.wait_recv()
        return s[n + "S"][y].astype(F32) + yy[0].astype(F32) + yy[1].astype(F32) + yy[2].astype(F32)

    def ag_ye(n):
        own_block = s[n + "G"].at[y, z]
        pending[n + "e"] = [rcopy(own_block, own_block, dev) for dev in y_devs]

    def ag_yf(n):
        for cp in pending[n + "e"]:
            cp.wait_recv()
        block = s[n + "G"].at[:, z]
        pending[n + "h"] = [rcopy(block, block, dev) for dev in z_devs]

    def ag_e(n):
        gr = s[n + "G"]
        own = gr.at[rows(f * 16, 16)]
        pending[n + "e"] = [rcopy(own, own, dev) for dev in z_devs]

    def ag_f(n):
        gr = s[n + "G"]
        for cp in pending[n + "e"]:
            cp.wait_recv()
        block = gr.at[rows(y * 64, 64)]
        pending[n + "f"] = [rcopy(block, block, dev_right), rcopy(block, block, dev_left)]

    def ag_h(n):
        gr = s[n + "G"]
        first, second = pending[n + "f"]
        first.wait_recv()
        one = gr.at[rows(left * 64, 32)]
        cps = [rcopy(one, one, dev_right)]
        second.wait_recv()
        two = gr.at[rows(right * 64 + 32, 32)]
        cps.append(rcopy(two, two, dev_left))
        pending[n + "h"] = cps

    def ag_i(n):
        for cp in pending[n + "h"]:
            cp.wait_recv()

    def ar_1(n):
        q = s[n + "Q"]
        pending[n + "1"] = rcopy(q.at[rows((1 - c) * 128, 128)], s[n + "AC"], c_dev)

    def ar_2(n):
        q, h1, ax = s[n + "Q"], s[n + "H1"], s[n + "AX"]
        pending[n + "1"].wait_recv()
        h1[...] = (q[rows(c * 128, 128)].astype(F32) + s[n + "AC"][...].astype(F32)).astype(BF)
        pending[n + "2"] = [
            rcopy(h1.at[rows(lax.rem(xh + d, 8) * 16, 16)], ax.at[d - 1], xh_devs[d - 1]) for d in range(1, 8)
        ]

    def ar_3(n):
        h1, ax, res = s[n + "H1"], s[n + "AX"], s[n + "R"]
        for cp in pending[n + "2"]:
            cp.wait_recv()
        total = h1[rows(xh * 16, 16)].astype(F32) + sum(ax[i].astype(F32) for i in range(7))
        at = rows(c * 128 + xh * 16, 16)
        res[at] = total.astype(BF)
        pending[n + "3"] = [rcopy(res.at[at], res.at[at], dev) for dev in xh_devs]

    def ar_4(n):
        res = s[n + "R"]
        for cp in pending[n + "3"]:
            cp.wait_recv()
        at = res.at[rows(c * 128, 128)]
        pending[n + "4"] = rcopy(at, at, c_dev)

    def ar_5(n):
        pending[n + "4"].wait_recv()
        return s[n + "R"][...].astype(F32)

    def ex_start(buf, value, slot, devs):
        one = buf.at[slot]
        one[0:2, :] = value[0:2, 0:128]
        one[2:4, :] = value[0:2, 128:256]
        return [rcopy(one, one, dev) for dev in devs]

    def ex_sum(buf, cps):
        for cp in cps:
            cp.wait_recv()
        total = sum(buf[i] for i in range(buf.shape[0]))
        return jnp.concatenate([total[0:2, :], total[2:4, :]], 1)

    row_id = lax.broadcasted_iota(jnp.int32, (8, W), 0)
    pick0 = jnp.where(row_id == 0, 1.0, 0.0).astype(F32)
    pick1 = jnp.where(row_id == 1, 1.0, 0.0).astype(F32)

    def pair_sums(first, second):
        return nt(pick0, first, precision=HIGH) + nt(pick1, second, precision=HIGH)

    loads["tok"].wait()
    inputs = s["tok"][...].astype(F32)
    stats = pair_sums(inputs, inputs * inputs)
    stat = s["st"].at[f]
    stat[0:2, :] = stats[0:2, 0:128]
    stat[2:4, :] = stats[0:2, 128:256]
    local = (inputs - jnp.mean(inputs, 1, keepdims=True))
    loads["gain"].wait()
    gain = s["gain"][...][None, :]
    local = (local * gain).astype(BF)
    gain_high = gain.astype(BF).astype(F32)
    row16 = lax.broadcasted_iota(jnp.int32, (16, W), 0)
    gain_rows = jnp.where(row16 == 0, gain_high, jnp.where(row16 == 1, gain - gain_high, 0.0)).astype(BF)
    wg = s["wg"].at[y]
    wz = s["wz"].at[z]

    def gain_product(weight):
        both = nn(gain_rows, weight)
        return both[0:1, :] + both[1:2, :]

    loads["aw"].wait()
    for i in range(3):
        line = gain_product(s["aw"][i])
        part = nn(local, s["aw"][i]).astype(BF)
        for k in HEADS:
            wg[3 * k + i : 3 * k + i + 1, :] = line[:, k * 128 : (k + 1) * 128]
        wz[i : i + 1, :] = line[:, 0:128]
        s["h0P"][:, :, :, i * 128 : (i + 1) * 128] = part[:, 0:128].reshape(4, 4, 16, 128)
        for k in (1, 2):
            s[f"h{k}P"][:, i * 128 : (i + 1) * 128] = part[:, k * 128 : (k + 1) * 128]
    loads["ups"].wait()
    loads["ow"].wait()
    ups = s["ups"][...]
    part = nt(ups, s["ow"][...]).astype(BF)
    s["h0P"][:, :, :, W:512] = part[:, 0:128].reshape(4, 4, 16, 128)
    for k in (1, 2):
        s[f"h{k}P"][:, W:512] = part[:, k * 128 : (k + 1) * 128]
    loads["uw"].wait()
    for i in range(4):
        line = gain_product(s["uw"][:, i * W : (i + 1) * W])
        for k in range(3):
            wg[9 + 3 * i + k : 10 + 3 * i + k, :] = line[:, k * 128 : (k + 1) * 128]

    def up_product(k):
        for i in range(0, UP[k][1], W):
            at = UP[k][0] + i
            s[f"u{k}P"][:, i : i + W] = nn(local, s["uw"][:, at : at + W]).astype(BF)

    def down_product(k):
        for i in range(0, UP[k][1], W):
            at = UP[k][0] + i
            s[f"d{k}P"][:, i : i + W] = nt(ups, s["dw"][at : at + W, :]).astype(BF)

    loads["dw"].wait()
    for k in (1, 0):
        up_product(k)
        down_product(k)
    own = rows(f * 16, 16)

    def head_rows(k):
        part = rs_d(f"h{k}") if k else rs_zd("h0")
        s[f"h{k}G"][own, 0:W] = (part[:, 0:W] * s["col"][own, 1:2]).astype(BF)
        s[f"h{k}G"][own, W:512] = part[:, W:512].astype(BF)
        ag_e(f"h{k}")

    def up_rows(k):
        part = rs_d(f"u{k}") * s["col"][own, 1:2]
        s["rawup"][:, UP[k][0] : UP[k][0] + UP[k][1]] = part
        s[f"a{k}G"][own, :] = gelu_value(part).astype(BF)
        ag_e(f"a{k}")

    def low_rows(k):
        part = rs_d(f"d{k}").astype(BF).astype(F32)
        part = (part * gelu_slope(s["rawup"][:, UP[k][0] : UP[k][0] + UP[k][1]])).astype(BF)
        if k == 0:
            s["l0G"][own, :] = part
            ag_e("l0")
        else:
            s["l1G"][y, z] = part
            ag_ye("l1")

    def gelu_value(v):
        return 0.5 * v * (1.0 + lax.erf(v * 0.7071067811865476))

    def gelu_slope(v):
        return (
            0.5 * (1.0 + lax.erf(v * 0.7071067811865476)) + v * jnp.exp(-0.5 * v * v) * 0.3989422804014327
        )

    score_scale = HEAD_DIM ** (-0.5)

    def head_norm(v):
        cent = v - jnp.mean(v, -1, keepdims=True)
        scale = lax.rsqrt(jnp.mean(cent * cent, -1, keepdims=True) + EPS)
        return cent * scale, scale

    def norm_back(gr, normed_v, scale):
        return scale * (
            gr - jnp.mean(gr, -1, keepdims=True) - normed_v * jnp.mean(gr * normed_v, -1, keepdims=True)
        )

    def head(i):
        lo = i * HEAD_DIM
        hi = lo + HEAD_DIM
        gr = s[f"h{i}G"]
        qn, qs = head_norm(gr[:, 0:128].astype(F32))
        kn, ks = head_norm(gr[:, 128:256].astype(F32))
        v = gr[:, 256:384]
        da = gr[:, 384:512]
        q, k = qn.astype(BF), kn.astype(BF)
        e = jnp.exp(nt(q, k) * score_scale)
        p = e / jnp.sum(e, -1, keepdims=True)
        pl_ = p.astype(BF)
        s["att"][:, lo:hi] = nn(pl_, v).astype(BF)
        dp = nt(da, v)
        ds = (p * (dp - jnp.sum(dp * p, -1, keepdims=True)) * score_scale).astype(BF)
        s["low"][0, :, lo:hi] = norm_back(nn(ds, k), qn, qs).astype(BF)
        s["low"][1, :, lo:hi] = norm_back(tn(ds, q), kn, ks).astype(BF)
        s["low"][2, :, lo:hi] = tn(pl_, da).astype(BF)

    pl.semaphore_wait(barrier, len(peers))
    rs_za("h0")
    rs_a("h2")
    rs_a("h1")
    st_cps = [rcopy(stat, stat, dev) for dev in fin_devs]
    wg_cps = [rcopy(wg, wg, dev) for dev in y_devs] + [rcopy(wz, wz, dev) for dev in z_devs]
    rs_a("u1")
    rs_b("h1")
    rs_b("h2")
    rs_a("d1")
    for cp in st_cps:
        cp.wait_recv()
    total = sum(s["st"][i] for i in range(16))
    mean_row = jnp.concatenate([total[0:1, :], total[2:3, :]], 1) / D
    square_row = jnp.concatenate([total[1:2, :], total[3:4, :]], 1) / D
    inv_row = lax.rsqrt(square_row - mean_row * mean_row + EPS)
    lines = [mean_row, inv_row]
    for i in range(8):
        one = s["st"][i * 4 + z] if i < 4 else s["st"][y * 4 + i - 4]
        lines.append(jnp.concatenate([one[0:1, :], one[2:3, :]], 1) / W - mean_row)
    lines += [mean_row] * 6
    s["col"][...] = jnp.concatenate(lines * 8, 0).T
    rs_b("u1")
    for cp in wg_cps:
        cp.wait_recv()
    rs_c("h1", (3, 4, 5))
    rs_a("u0")
    rs_c("h2", (6, 7, 8))
    rs_a("d0")
    rs_c("u1", tuple(range(15, 21)))
    rs_b("d1")
    head_rows(1)
    rs_b("u0")
    rs_b("d0")
    head_rows(2)
    rs_c("d1")
    rs_zc("h0", (0, 1, 2))
    rs_c("u0", tuple(range(9, 15)))
    ag_f("h1")
    up_rows(1)
    ag_f("h2")
    rs_c("d0")
    head_rows(0)
    up_rows(0)
    low_rows(1)
    ag_h("h1")
    ag_h("h2")
    centred = (inputs - s["col"][:, 0:1]) * s["col"][:, 1:2]
    s["cen"][...] = centred
    normed = (centred * gain).astype(BF)
    s["nrt"][...] = normed.T
    low_rows(0)
    ag_f("a1")
    ag_f("h0")
    ag_yf("l1")
    ag_f("a0")
    ag_f("l0")
    ag_h("a1")
    ag_i("h1")
    head(1)
    ag_h("h0")
    ag_h("a0")
    ag_i("h2")
    head(2)
    ag_h("l0")
    ag_i("h0")
    head(0)
    ag_i("a0")
    branch = nn(s["att"][...], s["ow"][...]) + nn(s["a0G"][...], s["dw"][0:WIDE, :])
    ag_i("a1")
    s["bQ"][...] = (branch + nn(s["a1G"][...], s["dw"][WIDE:FF, :])).astype(BF)
    ar_1("b")
    ngrad = nt(s["low"][0], s["aw"][0]) + nt(s["low"][1], s["aw"][1]) + nt(s["low"][2], s["aw"][2])
    ag_i("l0")
    s["ng"][...] = ngrad + nt(s["l0G"][...], s["uw"][:, 0:WIDE])
    ar_2("b")
    ag_i("l1")
    l1_rows = s["l1G"][...].reshape(T, NARROW)
    ngrad = s["ng"][...] + nt(l1_rows, s["uw"][:, WIDE:FF])
    s["nQ"][...] = ngrad.astype(BF)
    ar_1("n")
    scaled = ngrad * gain
    sums = pair_sums(scaled, scaled * s["cen"][...])
    sm_cps = ex_start(s["fa"], sums, f, fin_devs)
    ar_2("n")
    for i in range(3):
        s["ag_v"][i] = nn(s["nrt"][...], s["low"][i]).astype(BF)
    s["og_v"][...] = tn(s["att"][...], ups).astype(BF)
    ar_3("b")
    sums = ex_sum(s["fa"], sm_cps)
    sm_cps = ex_start(s["fb"], sums, c, [c_dev])
    ar_3("n")
    sums = ex_sum(s["fb"], sm_cps)
    sm_cps = ex_start(s["fc"], sums, xh, xh_devs)
    for i in (0, W):
        s["ug_v"][:, i : i + W] = nn(s["nrt"][...], s["l0G"][:, i : i + W]).astype(BF)
        s["ug_v"][:, WIDE + i : WIDE + i + W] = nn(s["nrt"][...], l1_rows[:, i : i + W]).astype(BF)
    ar_4("b")
    for i in (0, W):
        s["dg_v"][i : i + W, :] = tn(s["a0G"][:, i : i + W], ups).astype(BF)
        s["dg_v"][WIDE + i : WIDE + i + W, :] = tn(s["a1G"][:, i : i + W], ups).astype(BF)
    s["lo_v"][...] = (s["tok"][...].astype(F32) + ar_5("b")).astype(BF)
    ar_4("n")
    sums = ex_sum(s["fc"], sm_cps)
    columns = jnp.concatenate([sums] * 64, 0).T
    grad_mean = columns[:, 0:1] / D
    grad_cross = columns[:, 1:2] / D
    ngrad = ar_5("n")
    centred = s["cen"][...]
    s["gg_v"][...] = jnp.sum(ngrad * centred, 0)
    inner = ngrad * gain - grad_mean - centred * grad_cross
    s["tg_v"][...] = (ups.astype(F32) + s["col"][:, 1:2] * inner).astype(BF)

    for cp in copies:
        cp.wait_send()


def hand_on(*refs):
    sem = refs[-1]
    cps = [pltpu.make_async_copy(refs[i], refs[7 + i], sem.at[i]) for i in range(7)]
    for cp in cps:
        cp.start()
    for cp in cps:
        cp.wait()


def body(tokens, norm_gain, attend_weight, up_weight, out_weight, down_weight, upstream):
    any_spec = pl.BlockSpec(memory_space=pl.ANY)
    outs = pl.pallas_call(
        kernel,
        out_shape=(
            pltpu.VMEM((T, W), BF),
            pltpu.VMEM((T, W), BF),
            pltpu.VMEM((W,), F32),
            pltpu.VMEM((3, W, W), BF),
            pltpu.VMEM((W, FF), BF),
            pltpu.VMEM((W, W), BF),
            pltpu.VMEM((FF, W), BF),
        ),
        in_specs=[any_spec] * 7,
        out_specs=(pl.BlockSpec(memory_space=pltpu.VMEM),) * 7,
        scratch_shapes=[pltpu.VMEM(shape, dtype) for shape, dtype in SHAPES.values()]
        + [
            pltpu.SemaphoreType.DMA((N_COPIES,)),
            pltpu.SemaphoreType.DMA((N_COPIES,)),
            pltpu.SemaphoreType.DMA((8,)),
        ],
        compiler_params=pltpu.CompilerParams(
            collective_id=0, has_side_effects=True, vmem_limit_bytes=57 * 1024 * 1024
        ),
        name="layer",
    )(tokens, norm_gain, attend_weight, up_weight, out_weight, down_weight, upstream)
    return pl.pallas_call(
        hand_on,
        out_shape=tuple(jax.ShapeDtypeStruct(o.shape, o.dtype) for o in outs),
        in_specs=[any_spec] * 7,
        out_specs=(any_spec,) * 7,
        scratch_shapes=[pltpu.SemaphoreType.DMA((7,))],
        compiler_params=pltpu.CompilerParams(vmem_limit_bytes=2 * 1024 * 1024),
        name="hand_on",
    )(*outs)


def solution(mesh):
    return jax.shard_map(
        body,
        mesh=mesh,
        in_specs=(
            P(None, "fin"),
            P("fin"),
            P(None, "fin", "fout"),
            P("fin", "fout"),
            P("fout", "fin"),
            P("fout", "fin"),
            P(None, "fin"),
        ),
        out_specs=(
            P(None, "fin"),
            P(None, "fin"),
            P("fin"),
            P(None, "fin", "fout"),
            P("fin", "fout"),
            P("fout", "fin"),
            P("fout", "fin"),
        ),
        check_vma=False,
    )
```
